32 devices in a mesh: groups: 2 (over y), src: 16 (over z, x, core).
Axes of the slice: x: 2, y: 2, z: 4, core: 2. Of those that a mesh axis runs over, the one named last changes fastest.
Arguments:
- src_points: bfloat16 [256, 64, 256], P(('groups', 'src')), parts along dimension 0, may hold values from -1.5 to 1.5
- tgt_points: bfloat16 [256, 64, 256], P(('groups', 'src')), parts along dimension 0, may hold values from -1.5 to 1.5
- g_init: float32 [256, 256], P(('groups', 'src')), parts along dimension 0, may hold values from 2 to 66
- far_src: float32 [256, 256], P(('groups', 'src')), parts along dimension 0, may hold values from 10 to 22
- far_tgt: float32 [256, 256], P(('groups', 'src')), parts along dimension 0, may hold values from -160 to -14
- cand_owner: int32 [256, 8], P(('groups', 'src')), parts along dimension 0, may hold values from 0 to 15, all different within a row; in each aligned block of 8 rows (0 to 7, 8 to 15, ...) at most 4 rows name the same one
- cand_local: int32 [256, 8], P(('groups', 'src')), parts along dimension 0, may hold values from 0 to 7
Outputs:
- src_potential: float32 [256, 256], P(('groups', 'src')), parts along dimension 0
- tgt_potential: float32 [256, 256], P(('groups', 'src')), parts along dimension 0
The draws below stay inside these ranges and needn't reach their ends.
There are 2 independent parts, one for each index of `groups`. The reference program is written for one: setup_inputs(seed, part) draws one part's arguments, and reference() takes and returns one part's arrays. A program takes and returns all parts, laid end to end along the dimension named above; each array names one. Nothing has to cross between parts.
Inputs may be any that keep to these rules, and one draw needn't show every extreme that they name: `cand_owner`: each source cluster names 8 different shards; among the 8 source clusters of one device at most 4 name the same shard, and in every draw some device names some shard exactly 4 times.
All inputs are finite; a program needn't handle non-finite values.
Results may differ from the reference program's by a relative error of at most 0.0003.
Values may be sent and summed in bfloat16 or wider, within the bound.
No kernel may reach another device: no remote copies, remote signals or barrier semaphores. Data moves between devices by JAX's collectives and lax.ppermute only.
A program may use at most 64 MiB of HBM per device.

```python
import math
import jax
import jax.numpy as jnp
import numpy as np
from jax import lax

D = 64
PTS = 256
K = 8
ITERS = 2
SC_DEV = 8
TC_DEV = 8
CAP = 4
SC = 128
TC = 128
N_SRC = 16


def draw_g_init(key, part):
    base = jax.random.uniform(jax.random.fold_in(key, 1), (TC, PTS), jnp.float32, 2.0, 6.0)
    return base


def draw_far_tgt(key, part):
    base = jax.random.uniform(jax.random.fold_in(key, 3), (TC, PTS), jnp.float32, -26.0, -14.0)
    return base


def set_ends(result, stream_key, least, top_value):
    shape = result.shape
    place = [jax.random.randint(jax.random.fold_in(stream_key, axis), (), 0, shape[axis]) for axis in range(len(shape))]
    result = result.at[tuple(place)].set(least)
    longest = shape.index(max(shape))
    place[longest] = (place[longest] + 1) % shape[longest]
    return result.at[tuple(place)].set(top_value)


def steps_of(own_key, shape, split, low, largest):
    loudness = 1.0
    for position, blocks in split:
        steps = jax.random.uniform(jax.random.fold_in(jax.random.fold_in(own_key, 6), position), (blocks,), jnp.float32, low / len(split), largest / len(split))
        loudness = loudness * jnp.repeat(jnp.exp(steps), shape[position] // blocks).reshape((-1,) + (1,) * (len(shape) - 1 - position))
    return loudness


def shared_out(own_key, own, number, rows, number_of, top, limit, skew):
    order = jax.random.permutation(own_key, number_of)
    crowded, ordinary = load_shares(number_of, rows * top, limit, skew, True), load_shares(number_of, rows * top, limit, skew, False)
    places = jnp.arange(number_of)

    def named(sizes, rotation):
        used = int((sizes > 0).sum())
        fixed = max(1, used // 4)
        shifted = fixed + (places - fixed + rotation * (used - fixed)) % max(1, number_of - fixed)
        return jnp.zeros((number_of,), jnp.int32).at[order[jnp.where(places < fixed, places, shifted)]].set(jnp.asarray(sizes, jnp.int32))

    sizes = jnp.where(number % 4 == 0, named(crowded, number // 4), named(ordinary, number - number // 4 - 1))
    mixed = jax.random.permutation(jax.random.fold_in(own, 3), number_of)
    donor, taker = mixed[0:number_of // 2 * 2:2], mixed[1:number_of // 2 * 2:2]
    margin = jnp.minimum(sizes[donor] - 1, limit - sizes[taker]) // 2
    margin = jnp.where((donor == order[0]) | (taker == order[0]) | (sizes[taker] == 0), 0, jnp.maximum(margin, 0))
    shifted = jax.random.randint(jax.random.fold_in(own, 4), (number_of // 2,), 0, 1 << 20) % (margin + 1)
    sizes = sizes.at[donor].add(-shifted).at[taker].add(shifted)
    members = jnp.searchsorted(jnp.cumsum(sizes), jnp.arange(rows * top), side="right").astype(jnp.int32)
    table = members.reshape(top, rows).T
    table = table[jax.random.permutation(jax.random.fold_in(own, 1), rows)]
    rotation = jax.random.randint(jax.random.fold_in(own, 2), (rows, 1), 0, top)
    return jnp.take_along_axis(table, (jnp.arange(top)[None, :] + rotation) % top, axis=1)


def load_shares(amount, total, reach, lean, full):
    portions = [(1 << 20) // math.isqrt(standing ** lean) + 1 for standing in range(1, amount + 1)]
    largest = reach if full else min(reach, max(-(-total // amount), total * portions[0] // sum(portions)))
    least = 1 if total - largest >= amount - 1 else 0
    counts, surplus = [largest] + [least] * (amount - 1), total - largest - least * (amount - 1)
    while surplus > 0:
        free = [i for i in range(1, amount) if counts[i] < largest] or [i for i in range(1, amount) if counts[i] < reach]
        whole, left = sum([portions[i] for i in free]), surplus
        for i in free:
            more = min(reach - counts[i], max(1, left * portions[i] // whole), surplus)
            counts[i] = counts[i] + more
            surplus = surplus - more
    return np.array(counts)


def scatter_about(own_key, extent, scale, most, cuts=(), held_as=jnp.bfloat16):
    values = jax.random.normal(own_key, extent, jnp.float32) * scale
    if len(cuts) > 0:
        values = steps_of(own_key, extent, cuts, -0.22, 0.18) * values
    return jnp.clip(values, min=-most, max=most).astype(held_as)


def setup_inputs(seed: int = 0, part: int = 0) -> dict:
    keys = jax.random.split(jax.random.key(seed), 8)
    own_keys = jax.random.split(jax.random.fold_in(keys[7], part), 8)
    src_points = scatter_about(own_keys[0], (SC, D, PTS), 0.25, 1.5, ((0, 16),))
    tgt_points = scatter_about(own_keys[1], (TC, D, PTS), 0.25, 1.5, ((0, 16),))
    g_init = draw_g_init(jax.random.fold_in(jax.random.fold_in(keys[7], part), 71), part)
    far_src = jnp.clip(10.0 + 12.0 * jax.random.uniform(own_keys[3], (SC, PTS), jnp.float32) ** steps_of(own_keys[3], (SC, PTS), ((0, 16),), -0.2, 0.2), 10.0, 22.0)
    far_tgt = draw_far_tgt(jax.random.fold_in(jax.random.fold_in(keys[7], part), 71), part)
    cand_owner_keys = jax.random.split(jax.random.fold_in(own_keys[5], 1), SC // SC_DEV)
    cand_owner_turns = jax.random.permutation(jax.random.fold_in(own_keys[5], 3), SC // SC_DEV)
    cand_owner = jax.vmap(lambda own, number: shared_out(jax.random.fold_in(own_keys[5], 2), own, number, SC_DEV, N_SRC, K, CAP, 2))(cand_owner_keys, cand_owner_turns).reshape((SC, K))
    cand_local = set_ends(jax.random.randint(own_keys[6], (SC, K), 0, TC_DEV), jax.random.fold_in(own_keys[6], 1), 0, TC_DEV - 1).astype(jnp.int32)
    return {"src_points": src_points, "tgt_points": tgt_points, "g_init": g_init, "far_src": far_src, "far_tgt": far_tgt, "cand_owner": cand_owner, "cand_local": cand_local}


SCALE_EPS = 0.25
KEEP_TAU = 0.8


def half_norms(blocks):
    wide = blocks.astype(jnp.float32)
    return 0.5 * jnp.sum(wide * wide, axis=-2)


def reference(src_points, tgt_points, g_init, far_src, far_tgt, cand_owner, cand_local):
    cand = (cand_owner * TC_DEV + cand_local).astype(jnp.int32)
    src_half = half_norms(src_points)
    tgt_half = half_norms(tgt_points)
    indices = jnp.arange(SC, dtype=jnp.int32)

    def tile_cost(index):
        targets = cand[index]
        src_block = src_points[index].astype(jnp.float32)
        tgt_block = tgt_points[targets].astype(jnp.float32)
        inner = jnp.einsum("dp,kdq->pkq", src_block, tgt_block, precision=lax.Precision.HIGHEST)
        cost = src_half[index][:, None, None] + tgt_half[targets][None, :, :] - inner
        return cost, targets

    tgt_pot = g_init
    src_pot = jnp.zeros((SC, PTS), jnp.float32)
    for iteration in range(ITERS):
        def row_update(index):
            cost, targets = tile_cost(index)
            scores = (tgt_pot[targets][None, :, :] - cost) / SCALE_EPS
            far_term = far_src[index]
            highest = jnp.maximum(jnp.max(scores, axis=(1, 2)), far_term)
            total = jnp.exp(far_term - highest) + jnp.sum(jnp.exp(scores - highest[:, None, None]), axis=(1, 2))
            return -KEEP_TAU * SCALE_EPS * (highest + jnp.log(total))

        src_pot = lax.map(row_update, indices)

        def column_update(index):
            cost, targets = tile_cost(index)
            scores = (src_pot[index][:, None, None] - cost) / SCALE_EPS
            highest = jnp.max(scores, axis=0)
            total = jnp.sum(jnp.exp(scores - highest[None, :, :]), axis=0)
            return highest, total

        col_high, col_total = lax.map(column_update, indices)
        flat_ids = cand.reshape(SC * K)
        col_high = col_high.reshape(SC * K, PTS)
        col_total = col_total.reshape(SC * K, PTS)
        best = far_tgt.at[flat_ids].max(col_high)
        weights = col_total * jnp.exp(col_high - best[flat_ids])
        summed = jnp.exp(far_tgt - best).at[flat_ids].add(weights)
        tgt_pot = -KEEP_TAU * SCALE_EPS * (best + jnp.log(summed))
    return src_pot, tgt_pot
```

```python
import functools
import math

import jax
import jax.numpy as jnp
from jax import lax
from jax.experimental import pallas as pl
from jax.experimental.pallas import tpu as pltpu
from jax.sharding import PartitionSpec as P

ITERS = 2
SCALE_EPS = 0.25
KEEP_TAU = 0.8
INV_EPS = 1.0 / SCALE_EPS

LOW_OFFSET = 60.0
LOW_TOP = 130.0
HIGH_OFFSET = 200.0
COLUMN_TOP = -KEEP_TAU * 10.0
LOG_LARGEST = 88.4

DEPTH = 128
VMEM = 24 * 1024 * 1024


def split3(value):
    high = value.astype(jnp.bfloat16).astype(jnp.float32)
    rest = value - high
    mid = rest.astype(jnp.bfloat16).astype(jnp.float32)
    return high, mid, rest - mid


def prepare(points, place, count, state):
    clusters, dims, size = points.shape

    def body(points_ref, *refs):
        lhs_ref, rhs_ref, half_ref = refs[-3:]
        row = lax.broadcasted_iota(jnp.int32, (DEPTH - dims, size), 0)
        ones = jnp.where(row < 3, 1.0, 0.0).astype(jnp.float32)

        def one(c, carry):
            raw = points_ref[c]
            wide = raw.astype(jnp.float32)
            half = 0.5 * jnp.sum(wide * wide, axis=0, keepdims=True)
            half_ref[0, pl.ds(c, 1), :] = half
            high, mid, low = split3(-INV_EPS * half)
            extra = jnp.where(row == 0, high, jnp.where(row == 1, mid, jnp.where(row == 2, low, 0.0)))
            rhs_ref[0, c, :dims, :] = raw
            rhs_ref[0, c, dims:, :] = extra.astype(jnp.bfloat16)
            lhs_ref[0, c] = jnp.concatenate([INV_EPS * wide, ones], axis=0).T.astype(jnp.bfloat16)
            return carry

        lax.fori_loop(0, clusters, one, 0, unroll=2)

    shapes = (
        jax.ShapeDtypeStruct((count, clusters, size, DEPTH), jnp.bfloat16),
        jax.ShapeDtypeStruct((count, clusters, DEPTH, size), jnp.bfloat16),
        jax.ShapeDtypeStruct((count, clusters, size), jnp.float32),
    )
    extra_specs = [] if state is None else [pl.BlockSpec(memory_space=pl.ANY)] * 3
    return pl.pallas_call(
        body,
        grid=(1,),
        out_shape=shapes,
        in_specs=[pl.BlockSpec((clusters, dims, size), lambda i: (0, 0, 0))] + extra_specs,
        out_specs=(
            pl.BlockSpec((1, clusters, size, DEPTH), lambda i: (place, 0, 0, 0)),
            pl.BlockSpec((1, clusters, DEPTH, size), lambda i: (place, 0, 0, 0)),
            pl.BlockSpec((1, clusters, size), lambda i: (place, 0, 0)),
        ),
        input_output_aliases={} if state is None else {1: 0, 2: 1, 3: 2},
        compiler_params=pltpu.CompilerParams(vmem_limit_bytes=VMEM),
        cost_estimate=pl.CostEstimate(
            flops=clusters * dims * size * 4, bytes_accessed=clusters * size * DEPTH * 4, transcendentals=0
        ),
        name="prepare",
    )(points, *(() if state is None else state))


def swap_blocks(array, place, rows):
    blocks = array.shape[-2] // rows
    order = [q ^ (1 << place) for q in range(blocks)]
    return jnp.concatenate([array[..., q * rows:(q + 1) * rows, :] for q in order], axis=-2)


def list_pairs(me, cand, target_bits, tgt_count):
    sources, per_cluster = cand.shape
    group = tgt_count << len(target_bits)
    mask = sum(1 << b for b in target_bits)

    def body(me_ref, cand_ref, out_ref):
        own = me_ref[0]

        def one(s, filled):
            for k in range(per_cluster):
                code = cand_ref[s, k]
                apart = lax.div(code, tgt_count) ^ own
                block = 0
                for place, bit in enumerate(target_bits):
                    block = block | (((apart >> bit) & 1) << place)
                out_ref[filled + 1] = s * group + block * tgt_count + lax.rem(code, tgt_count)
                filled = filled + jnp.where((apart & ~mask) == 0, 1, 0).astype(jnp.int32)
            return filled

        out_ref[0] = lax.fori_loop(0, sources, one, jnp.int32(0))

    return pl.pallas_call(
        body,
        out_shape=jax.ShapeDtypeStruct((sources * per_cluster + 2,), jnp.int32),
        in_specs=[pl.BlockSpec(memory_space=pltpu.SMEM)] * 2,
        out_specs=pl.BlockSpec(memory_space=pltpu.SMEM),
        cost_estimate=pl.CostEstimate(flops=1000000, bytes_accessed=10000, transcendentals=0),
        name="list_pairs",
    )(me, cand)


def spread_columns(rows_value, column_ref):
    turned = rows_value.T
    for r in range(rows_value.shape[0]):
        column_ref[r] = jnp.broadcast_to(turned[:, r:r + 1], column_ref.shape[1:])


def tile_sums(lhs_ref, rhs_ref, column_ref, m, n, keep=None, shift=0.0):
    size = lhs_ref.shape[1]
    step = 64
    right = rhs_ref[n]
    total = None
    for start in range(0, size, step):
        product = jnp.dot(lhs_ref[m, start:start + step, :], right, preferred_element_type=jnp.float32)
        column = column_ref[m, start:start + step, :]
        term = product + jnp.concatenate([column] * (size // column.shape[1]), axis=1)
        value = jnp.exp(term - shift if keep is not None else term)
        if keep is not None:
            value = jnp.where(keep(term), value, 0.0)
        part = jnp.sum(value.reshape(step // 8, 8, size), axis=0)
        total = part if total is None else total + part
    return total


def row_kernel(group, first, place, rows, pairs_ref, lhs_ref, rhs_ref, half_ref, pot_ref, come_ref, far_ref, out_ref, column_ref, acc_ref):
    if first:
        pot = pot_ref[...]
    else:
        sums = pot_ref[...] + swap_blocks(come_ref[...], place, rows)
        pot = -KEEP_TAU * SCALE_EPS * (jnp.log(sums) - column_offset(group))
    spread_columns(INV_EPS * (pot - half_ref[...]) - LOW_OFFSET, column_ref)
    targets = lhs_ref.shape[0]
    count = pairs_ref[0]

    def run(keep, shift):
        acc_ref[...] = jnp.zeros_like(acc_ref)

        def one(p, carry):
            code = pairs_ref[p + 1]
            s, t = lax.div(code, targets), lax.rem(code, targets)
            acc_ref[s] += tile_sums(lhs_ref, rhs_ref, column_ref, t, s, keep, shift)
            return carry

        lax.fori_loop(0, count, one, 0)
        return jnp.sum(acc_ref[...], axis=1)

    def far_added(sums):
        own = far_ref.shape[0]
        return jnp.concatenate([sums[:own] + jnp.exp(far_ref[...] - LOW_OFFSET), sums[own:]], axis=0)

    if not first:
        out_ref[...] = far_added(run(None, 0.0))
        return
    narrow = jnp.max(pot) <= LOW_TOP * SCALE_EPS

    @pl.when(narrow)
    def _():
        out_ref[0] = far_added(run(None, 0.0))
        out_ref[1] = jnp.zeros(out_ref.shape[1:], jnp.float32)

    @pl.when(jnp.logical_not(narrow))
    def _():
        edge = LOW_TOP - LOW_OFFSET
        out_ref[0] = far_added(run(lambda term: term <= edge, 0.0))
        out_ref[1] = run(lambda term: term > edge, HIGH_OFFSET - LOW_OFFSET)


def column_offset(terms):
    return LOG_LARGEST - COLUMN_TOP - math.log(terms)


def column_kernel(terms, first, place, rows, pairs_ref, lhs_ref, rhs_ref, half_ref, sums_ref, come_ref, far_ref, out_ref, pot_ref, column_ref, acc_ref):
    sums = sums_ref[...] + swap_blocks(come_ref[...], place, rows)
    if first:
        low, high = sums[0], sums[1]
        low_log = jnp.log(low) + LOW_OFFSET
        high_log = jnp.where(high > 0.0, jnp.log(jnp.where(high > 0.0, high, 1.0)) + HIGH_OFFSET, -1e30)
        top = jnp.maximum(low_log, high_log)
        log_sum = top + jnp.log(jnp.exp(low_log - top) + jnp.exp(high_log - top))
    else:
        log_sum = jnp.log(sums) + LOW_OFFSET
    pot = -KEEP_TAU * SCALE_EPS * log_sum
    pot_ref[...] = pot[:pot_ref.shape[0]]
    spread_columns(INV_EPS * (pot - half_ref[...]) + column_offset(terms), column_ref)
    targets = rhs_ref.shape[0]
    acc_ref[...] = jnp.zeros_like(acc_ref)

    def one(p, carry):
        code = pairs_ref[p + 1]
        s, t = lax.div(code, targets), lax.rem(code, targets)
        acc_ref[t] += tile_sums(lhs_ref, rhs_ref, column_ref, s, t)
        return carry

    lax.fori_loop(0, pairs_ref[0], one, 0)
    total = jnp.sum(acc_ref[...], axis=1)
    own = far_ref.shape[0]
    out_ref[...] = jnp.concatenate([total[:own] + jnp.exp(far_ref[...] + column_offset(terms)), total[own:]], axis=0)


def run_pass(kernel, out_shapes, lhs, rhs, pairs, tiles, *rest):
    size = lhs.shape[1]
    space = pl.BlockSpec(memory_space=pltpu.VMEM)
    return pl.pallas_call(
        kernel,
        out_shape=out_shapes,
        in_specs=[pl.BlockSpec(memory_space=pltpu.SMEM)] + [space] * (2 + len(rest)),
        out_specs=jax.tree.map(lambda _: space, out_shapes),
        scratch_shapes=[
            pltpu.VMEM((lhs.shape[0], size, 128), jnp.float32),
            pltpu.VMEM((rhs.shape[0], 8, size), jnp.float32),
        ],
        compiler_params=pltpu.CompilerParams(vmem_limit_bytes=VMEM),
        cost_estimate=pl.CostEstimate(
            flops=2 * tiles * size * size * DEPTH, bytes_accessed=8 << 20, transcendentals=tiles * size * size
        ),
        name="tiles",
    )(pairs, lhs, rhs, *rest)


def per_device(src_points, tgt_points, g_init, far_src, far_tgt, cand_owner, cand_local):
    src_count, _, size = src_points.shape
    tgt_count = tgt_points.shape[0]
    per_cluster = cand_owner.shape[1]
    shards = lax.axis_size("src")
    bits = shards.bit_length() - 1
    upper = max(bits // 2 - 1, 0)
    source_bits = [b for b in range(bits - 1, bits - 1 - upper, -1)] + [0]
    target_bits = [b for b in range(bits - 1 - upper, 0, -1)]
    nr, nc = 1 << len(source_bits), 1 << len(target_bits)
    capacity = max(2, min(src_count // 2, 2 * src_count * per_cluster // shards))
    terms = shards * capacity * size

    def across(array, bit):
        return lax.ppermute(array, "src", [(i, i ^ (1 << bit)) for i in range(shards)])

    def gathered(array, which):
        blocks = [array]
        for bit in which:
            blocks = blocks + [across(b, bit) for b in blocks]
        return blocks

    def grown(array, which):
        for bit in which:
            array = jnp.concatenate([array, across(array, bit)], axis=0)
        return array

    def added(array, which, rows):
        for place, bit in enumerate(which[:-1]):
            array = array + swap_blocks(across(array, bit), place, rows)
        return array, across(array, which[-1]), len(which) - 1

    cand = grown(cand_owner * tgt_count + cand_local, source_bits)
    pot = grown(g_init, target_bits)
    src_blocks = gathered(src_points, source_bits)
    tgt_blocks = gathered(tgt_points, target_bits)
    me = lax.axis_index("src").astype(jnp.int32).reshape(1)
    pairs = list_pairs(me, cand, target_bits, tgt_count)

    src_state = tgt_state = None
    for place, block in enumerate(src_blocks):
        src_state = prepare(block, place, nr, src_state)
    for place, block in enumerate(tgt_blocks):
        tgt_state = prepare(block, place, nc, tgt_state)
    src_lhs, src_rhs, src_half = [a.reshape((-1,) + a.shape[2:]) for a in src_state]
    tgt_lhs, tgt_rhs, tgt_half = [a.reshape((-1,) + a.shape[2:]) for a in tgt_state]

    f32 = jnp.float32
    sources, targets = nr * src_count, nc * tgt_count
    tiles = src_count * per_cluster
    come, place = pot, 0
    for iteration in range(ITERS):
        first = iteration == 0
        shape = (2, sources, size) if first else (sources, size)
        sums = run_pass(
            functools.partial(row_kernel, terms, first, place, tgt_count),
            jax.ShapeDtypeStruct(shape, f32),
            tgt_lhs, src_rhs, pairs, tiles, tgt_half, pot, come, far_src,
        )
        sums, come, place = added(sums, source_bits, src_count)
        column, src_pot = run_pass(
            functools.partial(column_kernel, terms, first, place, src_count),
            (jax.ShapeDtypeStruct((targets, size), f32), jax.ShapeDtypeStruct((src_count, size), f32)),
            src_lhs, tgt_rhs, pairs, tiles, src_half, sums, come, far_tgt,
        )
        pot, come, place = added(column, target_bits, tgt_count)
    other = (1 << place) * tgt_count
    total = pot[:tgt_count] + come[other:other + tgt_count]
    tgt_pot = -KEEP_TAU * SCALE_EPS * (jnp.log(total) - column_offset(terms))
    return (src_pot, tgt_pot)


def solution(mesh):
    return jax.shard_map(
        per_device,
        mesh=mesh,
        in_specs=(
            P(("groups", "src"), None, None),
            P(("groups", "src"), None, None),
            P(("groups", "src"), None),
            P(("groups", "src"), None),
            P(("groups", "src"), None),
            P(("groups", "src"), None),
            P(("groups", "src"), None),
        ),
        out_specs=(P(("groups", "src"), None), P(("groups", "src"), None)),
        check_vma=False,
    )
```

```python
import functools
import math

import jax
import jax.numpy as jnp
from jax import lax
from jax.experimental import pallas as pl
from jax.experimental.pallas import tpu as pltpu
from jax.sharding import PartitionSpec as P

ITERS = 2
SCALE_EPS = 0.25
KEEP_TAU = 0.8
INV_EPS = 1.0 / SCALE_EPS

LOW_OFFSET = 60.0
LOW_TOP = 130.0
HIGH_OFFSET = 200.0
COLUMN_TOP = -KEEP_TAU * 10.0
LOG_LARGEST = 88.4

NOTHING = -1e30

DEPTH = 128
GROUP = 64
EXTRA = 32
VMEM = 12 * 1024 * 1024
SMALL = 1024 * 1024
LARGE = 60 * 1024 * 1024


def split3(value):
    high = value.astype(jnp.bfloat16).astype(jnp.float32)
    rest = value - high
    mid = rest.astype(jnp.bfloat16).astype(jnp.float32)
    return high, mid, rest - mid


def pack(points, *rows):
    clusters, dims, size = points[0].shape
    counts = [len(r) for r in rows]
    tall = clusters * dims

    flat = [p.reshape(tall, size) for p in points]
    few = [r for r in rows for r in r]

    def body(*refs):
        points_refs, refs = refs[:len(points)], refs[len(points):]
        few_refs, refs = refs[:len(few)], refs[len(few):]
        out_refs, refs = refs[:len(points)], refs[len(points):]
        held_refs, sems = refs[:-1], refs[-1]
        copies = [pltpu.make_async_copy(p, o.at[:tall], sems.at[i]) for i, (p, o) in enumerate(zip(points_refs, out_refs))]
        loads = [pltpu.make_async_copy(f, h, sems.at[len(copies) + i]) for i, (f, h) in enumerate(zip(few_refs, held_refs))]
        for copy in loads + copies:
            copy.start()
        for copy in loads:
            copy.wait()
        held = list(held_refs)
        for i, n in enumerate(counts):
            mine, held = held[:n], held[n:]
            if n > 1:
                values = [ref[...].astype(jnp.float32) for ref in mine]
                values = [jnp.concatenate([v, jnp.zeros((v.shape[0], size - v.shape[1]), jnp.float32)], axis=1) for v in values]
            else:
                values = list(split3(mine[0][...]))
            empty = EXTRA - sum(v.shape[0] for v in values)
            if empty:
                values.append(jnp.zeros((empty, size), jnp.float32))
            out_refs[i][tall:, :] = jnp.concatenate(values, axis=0).astype(jnp.bfloat16)
        for copy in copies:
            copy.wait()

    return pl.pallas_call(
        body,
        out_shape=[jax.ShapeDtypeStruct((tall + EXTRA, size), p.dtype) for p in points],
        in_specs=[pl.BlockSpec(memory_space=pltpu.HBM)] * (len(points) + len(few)),
        out_specs=[pl.BlockSpec(memory_space=pltpu.VMEM)] * len(points),
        scratch_shapes=[pltpu.VMEM(f.shape, f.dtype) for f in few] + [pltpu.SemaphoreType.DMA((len(points) + len(few),))],
        compiler_params=pltpu.CompilerParams(vmem_limit_bytes=LARGE),
        name="pack",
    )(*flat, *few)


def prepare(blocks, clusters, count, state):
    rows, size = blocks[0][0].shape
    tall = rows - EXTRA
    dims = tall // clusters
    places = [place for _, place in blocks]

    def body(*refs):
        points_refs = refs[:len(blocks)]
        lhs_ref, rhs_ref, half_ref, extra_ref = refs[-4:]
        row = lax.broadcasted_iota(jnp.int32, (DEPTH - dims, size), 0)
        ones = jnp.where(row < 3, 1.0, 0.0).astype(jnp.float32)

        def write(points_ref):
            extra = points_ref[tall:, :].astype(jnp.float32)
            extra_ref[0] = extra[:clusters] + extra[clusters:2 * clusters] + extra[2 * clusters:3 * clusters]

            def one(c, carry):
                raw = points_ref[pl.ds(pl.multiple_of(c * dims, dims), dims), :]
                wide = raw.astype(jnp.float32)
                half = 0.5 * jnp.sum(wide * wide, axis=0, keepdims=True)
                half_ref[0, pl.ds(c, 1), :] = half
                high, mid, low = split3(-INV_EPS * half)
                extra = jnp.where(row == 0, high, jnp.where(row == 1, mid, jnp.where(row == 2, low, 0.0)))
                rhs_ref[0, c, :dims, :] = raw
                rhs_ref[0, c, dims:, :] = extra.astype(jnp.bfloat16)
                lhs_ref[0, c] = jnp.concatenate([INV_EPS * wide, ones], axis=0).T.astype(jnp.bfloat16)
                return carry

            lax.fori_loop(0, clusters, one, 0, unroll=2)

        for i, points_ref in enumerate(points_refs):
            pl.when(pl.program_id(0) == i)(functools.partial(write, points_ref))

    def place_of(i):
        chosen = places[0]
        for j, place in enumerate(places[1:]):
            chosen = jnp.where(i > j, place, chosen)
        return chosen

    shapes = (
        jax.ShapeDtypeStruct((count, clusters, size, DEPTH), jnp.bfloat16),
        jax.ShapeDtypeStruct((count, clusters, DEPTH, size), jnp.bfloat16),
        jax.ShapeDtypeStruct((count, clusters, size), jnp.float32),
        jax.ShapeDtypeStruct((count, clusters, size), jnp.float32),
    )
    used = len(blocks)
    extra_specs = [] if state is None else [pl.BlockSpec(memory_space=pl.ANY)] * 4
    return pl.pallas_call(
        body,
        grid=(used,),
        out_shape=shapes,
        in_specs=[pl.BlockSpec((rows, size), lambda i: (0, 0))] * used + extra_specs,
        out_specs=(
            pl.BlockSpec((1, clusters, size, DEPTH), lambda i: (place_of(i), 0, 0, 0)),
            pl.BlockSpec((1, clusters, DEPTH, size), lambda i: (place_of(i), 0, 0, 0)),
            pl.BlockSpec((1, clusters, size), lambda i: (place_of(i), 0, 0)),
            pl.BlockSpec((1, clusters, size), lambda i: (place_of(i), 0, 0)),
        ),
        input_output_aliases={} if state is None else {used + i: i for i in range(4)},
        compiler_params=pltpu.CompilerParams(vmem_limit_bytes=VMEM),
        cost_estimate=pl.CostEstimate(
            flops=used * clusters * dims * size * 4, bytes_accessed=used * clusters * size * DEPTH * 8, transcendentals=0
        ),
        name="prepare",
    )(*[points for points, _ in blocks], *(() if state is None else state))


def list_pairs(entries):
    rows, width = entries.shape

    def body(entries_ref, out_ref):
        def one(r, filled):
            for k in range(width):
                entry = entries_ref[r, k]
                out_ref[filled] = entry
                filled = filled + jnp.where(entry >= 0, 1, 0).astype(jnp.int32)
            return filled

        filled = lax.fori_loop(0, rows - 1, one, jnp.int32(1))
        out_ref[0] = filled - 1
        last = entries_ref[rows - 1, 0]
        for extra in range(GROUP):
            out_ref[filled + extra] = last

    return pl.pallas_call(
        body,
        out_shape=jax.ShapeDtypeStruct((rows * width + 1 + GROUP,), jnp.int32),
        in_specs=[pl.BlockSpec(memory_space=pltpu.SMEM)],
        out_specs=pl.BlockSpec(memory_space=pltpu.SMEM),
        compiler_params=pltpu.CompilerParams(vmem_limit_bytes=SMALL),
        cost_estimate=pl.CostEstimate(flops=0, bytes_accessed=4 << 20, transcendentals=0),
        name="list_pairs",
    )(entries)


def padded_rows(rows):
    return -(-3 * rows // 128) * 128


def sum_pairs(pairs_ref, lhs_ref, rhs_ref, sources, values, extra_ref, acc_ref, by_source, adjust=lambda term: term):
    size = lhs_ref.shape[1]
    targets = lhs_ref.shape[0] - sources
    count, others = (targets, sources) if by_source else (sources, targets)
    lhs_base, rhs_base = (sources, 0) if by_source else (0, sources)
    wide = extra_ref.shape[1]
    parts = list(split3(values))
    if wide > 3 * count:
        parts.append(jnp.zeros((wide - 3 * count, size), jnp.float32))
    extra_ref[...] = jnp.concatenate(parts, axis=0).T.astype(jnp.bfloat16)
    acc_ref[...] = jnp.zeros_like(acc_ref)
    row = lax.broadcasted_iota(jnp.int32, (wide, size), 0)
    row = jnp.where(row < 3 * count, lax.rem(row, count), count)

    def step(g, carry):
        for u in range(GROUP):
            code = pairs_ref[g * GROUP + u + 1]
            s, t = lax.div(code, 2 * targets), lax.rem(code, 2 * targets)
            m, place = (t, s) if by_source else (s, t)
            m, n = jnp.minimum(m, count - 1), jnp.minimum(place, others - 1)
            chosen = jnp.where(row == m, 1.0, 0.0).astype(jnp.bfloat16)
            term = jnp.dot(
                jnp.concatenate([lhs_ref[lhs_base + m], extra_ref[...]], axis=1),
                jnp.concatenate([rhs_ref[rhs_base + n], chosen], axis=0),
                preferred_element_type=jnp.float32,
            )
            acc_ref[place] += jnp.sum(jnp.exp(adjust(term)).reshape(size // 8, 8, size), axis=0)
        return carry

    lax.fori_loop(0, lax.div(pairs_ref[0] + (GROUP - 1), GROUP), step, 0)
    return jnp.sum(acc_ref[:others], axis=1)


def moved(block, home, rows):
    return pl.ds(pl.multiple_of((block ^ home) * rows, rows), rows)


def store_sums(sums, home, out_ref, far):
    rows = far.shape[0]
    for block in range(sums.shape[0] // rows):
        part = sums[block * rows:(block + 1) * rows]
        out_ref[moved(block, home, rows), :] = part + far if block == 0 else part


def load_sums(sums_refs, home, rows):
    blocks = []
    for block in range(sums_refs[0].shape[-2] // rows):
        blocks.append(sum(ref[moved(block, home, rows), :] for ref in sums_refs))
    return jnp.concatenate(blocks, axis=0)


def row_kernel(terms, sources, first, pairs_ref, home_ref, lhs_ref, rhs_ref, half_ref, far_ref, *refs):
    pot_refs, (out_ref, extra_ref, acc_ref) = refs[:-3], refs[-3:]
    if first:
        pot = pot_refs[0][sources:, :]
    else:
        pot = -KEEP_TAU * SCALE_EPS * (jnp.log(load_sums(pot_refs, home_ref[1], far_ref.shape[0])) - column_offset(terms))
    values = INV_EPS * (pot - half_ref[sources:, :]) - LOW_OFFSET
    run = functools.partial(sum_pairs, pairs_ref, lhs_ref, rhs_ref, sources, values, extra_ref, acc_ref, True)
    far = jnp.exp(far_ref[...] - LOW_OFFSET)
    if not first:
        store_sums(run(), home_ref[0], out_ref, far)
        return
    own = far_ref.shape[0]

    def store_logs(low, high=None):
        low = jnp.concatenate([low[:own] + far, low[own:]], axis=0)
        logs = log_or_nothing(low) + LOW_OFFSET
        if high is not None:
            high = log_or_nothing(high) + HIGH_OFFSET
            top = jnp.maximum(logs, high)
            logs = top + jnp.log(jnp.exp(logs - top) + jnp.exp(high - top))
        store_sums(logs, home_ref[0], out_ref, jnp.zeros_like(far))

    narrow = jnp.max(pot) <= LOW_TOP * SCALE_EPS

    @pl.when(narrow)
    def _():
        store_logs(run())

    @pl.when(jnp.logical_not(narrow))
    def _():
        edge = LOW_TOP - LOW_OFFSET
        low = run(lambda term: jnp.where(term <= edge, term, NOTHING))
        store_logs(low, run(lambda term: jnp.where(term > edge, term - (HIGH_OFFSET - LOW_OFFSET), NOTHING)))


def log_or_nothing(value):
    return jnp.where(value > 0.0, jnp.log(jnp.where(value > 0.0, value, 1.0)), NOTHING)


def column_offset(terms):
    return LOG_LARGEST - COLUMN_TOP - math.log(terms)


def column_kernel(terms, sources, first, pairs_ref, home_ref, lhs_ref, rhs_ref, half_ref, far_ref, sums_ref, out_ref, pot_ref, extra_ref, acc_ref):
    parts, own = range(sums_ref.shape[0]), pot_ref.shape[0]
    if first:
        logs = [load_sums([sums_ref.at[i]], home_ref[0], own) for i in parts]
        top = functools.reduce(jnp.maximum, logs)
        log_sum = top + jnp.log(sum(jnp.exp(log - top) for log in logs))
    else:
        log_sum = jnp.log(load_sums([sums_ref.at[i] for i in parts], home_ref[0], own)) + LOW_OFFSET
    pot = -KEEP_TAU * SCALE_EPS * log_sum
    values = INV_EPS * (pot - half_ref[:sources, :]) + column_offset(terms)
    total = sum_pairs(pairs_ref, lhs_ref, rhs_ref, sources, values, extra_ref, acc_ref, False)
    store_sums(total, home_ref[1], out_ref, jnp.exp(far_ref[...] + column_offset(terms)))
    pot_ref[...] = pot[:own]


def run_pass(kernel, out_shapes, pairs, home, state, width, others, tiles, *rest):
    size = state[0].shape[1]
    space = pl.BlockSpec(memory_space=pltpu.VMEM)
    return pl.pallas_call(
        kernel,
        out_shape=out_shapes,
        in_specs=[pl.BlockSpec(memory_space=pltpu.SMEM)] * 2 + [space] * (3 + len(rest)),
        out_specs=jax.tree.map(lambda _: space, out_shapes),
        scratch_shapes=[
            pltpu.VMEM((size, padded_rows(width)), jnp.bfloat16),
            pltpu.VMEM((others + 1, 8, size), jnp.float32),
        ],
        compiler_params=pltpu.CompilerParams(vmem_limit_bytes=VMEM),
        cost_estimate=pl.CostEstimate(
            flops=2 * tiles * size * size * DEPTH, bytes_accessed=8 << 20, transcendentals=tiles * size * size
        ),
        name="tiles",
    )(pairs, home, *state, *rest)


def per_device(src_points, tgt_points, g_init, far_src, far_tgt, cand_owner, cand_local):
    src_count, _, size = src_points.shape
    tgt_count = tgt_points.shape[0]
    per_cluster = cand_owner.shape[1]
    shards = lax.axis_size("src")
    bits = shards.bit_length() - 1
    upper = max(bits // 2 - 1, 0)
    source_bits = [0] + [b for b in range(bits - upper, bits)]
    target_bits = [b for b in range(1, bits - upper)]
    nr, nc = 1 << len(source_bits), 1 << len(target_bits)
    capacity = max(2, min(src_count // 2, 2 * src_count * per_cluster // shards))
    terms = shards * capacity * size

    def across(array, *which):
        apart = sum(1 << bit for bit in which)
        return lax.ppermute(array, "src", [(i, i ^ apart) for i in range(shards)])

    def doubled(array, which):
        blocks = {0: array}
        for place, bit in reversed(list(enumerate(which))):
            blocks.update({at | 1 << place: across(block, bit) for at, block in list(blocks.items())})
        return [blocks[at] for at in range(1 << len(which))]

    def groups(which):
        masks = [sum(1 << bit for place, bit in enumerate(which) if i >> place & 1) for i in range(1 << len(which))]
        return [[base | m for m in masks] for base in range(shards) if not base & sum(1 << b for b in which)]

    def place_of(device, which):
        return sum(((device >> bit) & 1) << place for place, bit in enumerate(which))

    tall = src_count * src_points.shape[1]
    sources, targets = nr * src_count, nc * tgt_count
    me = lax.axis_index("src").astype(jnp.int32)
    home = jnp.stack([place_of(me, source_bits), place_of(me, target_bits)])
    src_message, tgt_message = pack((src_points, tgt_points), (cand_owner, cand_local), (g_init,))
    src_blocks = doubled(src_message, source_bits)
    tgt_blocks = doubled(tgt_message, target_bits)
    state = None
    order = lambda blocks: sorted(range(len(blocks)), key=lambda at: (at.bit_count(), at))
    src_order, tgt_order = order(src_blocks), order(tgt_blocks)
    for i in range(max(nr, nc)):
        blocks = [(src_blocks[at], at) for at in src_order[i:i + 1]] + [(tgt_blocks[at], nr + at) for at in tgt_order[i:i + 1]]
        state = prepare(blocks, src_count, nr + nc, state)
    *state, extra = [a.reshape((-1,) + a.shape[2:]) for a in state]

    owner = jnp.concatenate([b[tall:tall + src_count, :per_cluster] for b in src_blocks], axis=0).astype(jnp.int32)
    local = jnp.concatenate([b[tall + src_count:tall + 2 * src_count, :per_cluster] for b in src_blocks], axis=0).astype(jnp.int32)
    inside = ((owner ^ me) & ~sum(1 << b for b in target_bits)) == 0
    row = lax.broadcasted_iota(jnp.int32, (sources, per_cluster), 0)
    entries = jnp.where(inside, row * (2 * targets) + place_of(owner ^ me, target_bits) * tgt_count + local, -1)
    nobody = jnp.full((1, per_cluster), sources * (2 * targets) + targets, jnp.int32)
    pairs = list_pairs(jnp.concatenate([entries, nobody], axis=0))
    pots = [extra]

    f32 = jnp.float32
    tiles = src_count * per_cluster
    for iteration in range(ITERS):
        first = iteration == 0
        sums = run_pass(
            functools.partial(row_kernel, terms, sources, first),
            jax.ShapeDtypeStruct((sources, size), f32),
            pairs, home, state, targets, sources, tiles, far_src, *pots,
        )
        sums = lax.all_gather(sums, "src", axis_index_groups=groups(source_bits))
        column, src_pot = run_pass(
            functools.partial(column_kernel, terms, sources, first),
            (jax.ShapeDtypeStruct((targets, size), f32), jax.ShapeDtypeStruct((src_count, size), f32)),
            pairs, home, state, sources, targets, tiles, far_tgt, sums,
        )
        if iteration + 1 < ITERS:
            for bit in target_bits[:-1]:
                column = column + across(column, bit)
            pots = [column, across(column, target_bits[-1])]
    column = lax.all_to_all(
        column.reshape(nc, tgt_count, size), "src", 0, 0, tiled=True, axis_index_groups=groups(target_bits)
    )
    tgt_pot = -KEEP_TAU * SCALE_EPS * (jnp.log(jnp.sum(column, axis=0)) - column_offset(terms))
    return (src_pot, tgt_pot)


def solution(mesh):
    return jax.shard_map(
        per_device,
        mesh=mesh,
        in_specs=(
            P(("groups", "src"), None, None),
            P(("groups", "src"), None, None),
            P(("groups", "src"), None),
            P(("groups", "src"), None),
            P(("groups", "src"), None),
            P(("groups", "src"), None),
            P(("groups", "src"), None),
        ),
        out_specs=(P(("groups", "src"), None), P(("groups", "src"), None)),
        check_vma=False,
    )
```

```python
import functools
import math

import jax
import jax.numpy as jnp
from jax import lax
from jax.experimental import pallas as pl
from jax.experimental.pallas import tpu as pltpu
from jax.sharding import PartitionSpec as P

ITERS = 2
SCALE_EPS = 0.25
KEEP_TAU = 0.8
INV_EPS = 1.0 / SCALE_EPS

LOW_OFFSET = 60.0
LOW_TOP = 130.0
HIGH_OFFSET = 200.0
COLUMN_TOP = -KEEP_TAU * 10.0
LOG_LARGEST = 88.4

NOTHING = -1e30
ALL, EARLY, LATE = range(3)

DEPTH = 128
GROUP = 64
PART = 16
EXTRA = 32
VMEM = 12 * 1024 * 1024
SMALL = 1024 * 1024
LARGE = 60 * 1024 * 1024


def split3(value):
    high = value.astype(jnp.bfloat16).astype(jnp.float32)
    rest = value - high
    mid = rest.astype(jnp.bfloat16).astype(jnp.float32)
    return high, mid, rest - mid


def pack(points, *rows):
    clusters, dims, size = points[0].shape
    counts = [len(r) for r in rows]
    tall = clusters * dims

    flat = [p.reshape(tall, size) for p in points]
    few = [r for r in rows for r in r]

    def body(*refs):
        points_refs, refs = refs[:len(points)], refs[len(points):]
        few_refs, refs = refs[:len(few)], refs[len(few):]
        out_refs, refs = refs[:len(points)], refs[len(points):]
        held_refs, sems = refs[:-1], refs[-1]
        copies = [pltpu.make_async_copy(p, o.at[:tall], sems.at[i]) for i, (p, o) in enumerate(zip(points_refs, out_refs))]
        loads = [pltpu.make_async_copy(f, h, sems.at[len(copies) + i]) for i, (f, h) in enumerate(zip(few_refs, held_refs))]
        for copy in loads + copies:
            copy.start()
        for copy in loads:
            copy.wait()
        held = list(held_refs)
        for i, n in enumerate(counts):
            mine, held = held[:n], held[n:]
            if n > 1:
                values = [ref[...].astype(jnp.float32) for ref in mine]
                values = [jnp.concatenate([v, jnp.zeros((v.shape[0], size - v.shape[1]), jnp.float32)], axis=1) for v in values]
            else:
                values = list(split3(mine[0][...]))
            empty = EXTRA - sum(v.shape[0] for v in values)
            if empty:
                values.append(jnp.zeros((empty, size), jnp.float32))
            out_refs[i][tall:, :] = jnp.concatenate(values, axis=0).astype(jnp.bfloat16)
        for copy in copies:
            copy.wait()

    return pl.pallas_call(
        body,
        out_shape=[jax.ShapeDtypeStruct((tall + EXTRA, size), p.dtype) for p in points],
        in_specs=[pl.BlockSpec(memory_space=pltpu.HBM)] * (len(points) + len(few)),
        out_specs=[pl.BlockSpec(memory_space=pltpu.VMEM)] * len(points),
        scratch_shapes=[pltpu.VMEM(f.shape, f.dtype) for f in few] + [pltpu.SemaphoreType.DMA((len(points) + len(few),))],
        compiler_params=pltpu.CompilerParams(vmem_limit_bytes=LARGE),
        name="pack",
    )(*flat, *few)


def prepare(blocks, clusters, dims, counts, state, after=()):
    size = blocks[0][0].shape[1]
    tall = clusters * dims
    places = [place for _, place in blocks]
    used = len(blocks)
    told = [place - counts[0] for place in places if place >= counts[0]]

    def body(*refs):
        points_refs = refs[:used]
        lhs_ref, rhs_ref, half_ref = refs[-4:-1] if told else refs[-3:]
        row = lax.broadcasted_iota(jnp.int32, (DEPTH - dims, size), 0)
        ones = jnp.where(row < 3, 1.0, 0.0).astype(jnp.float32)

        def write(points_ref, place):
            if place >= counts[0]:
                extra = points_ref[tall:, :].astype(jnp.float32)
                refs[-1][0] = extra[:clusters] + extra[clusters:2 * clusters] + extra[2 * clusters:3 * clusters]

            def one(c, carry):
                raw = points_ref[pl.ds(pl.multiple_of(c * dims, dims), dims), :]
                wide = raw.astype(jnp.float32)
                half = 0.5 * jnp.sum(wide * wide, axis=0, keepdims=True)
                half_ref[0, pl.ds(c, 1), :] = half
                high, mid, low = split3(-INV_EPS * half)
                extra = jnp.where(row == 0, high, jnp.where(row == 1, mid, jnp.where(row == 2, low, 0.0)))
                rhs_ref[0, c, :dims, :] = raw
                rhs_ref[0, c, dims:, :] = extra.astype(jnp.bfloat16)
                lhs_ref[0, c] = jnp.concatenate([INV_EPS * wide, ones], axis=0).T.astype(jnp.bfloat16)
                return carry

            lax.fori_loop(0, clusters, one, 0, unroll=2)

        for i, points_ref in enumerate(points_refs):
            pl.when(pl.program_id(0) == i)(functools.partial(write, points_ref, places[i]))

    def place_of(i):
        chosen = places[0]
        for j, place in enumerate(places[1:]):
            chosen = jnp.where(i > j, place, chosen)
        return chosen

    count = sum(counts)
    shapes = [
        jax.ShapeDtypeStruct((count, clusters, size, DEPTH), jnp.bfloat16),
        jax.ShapeDtypeStruct((count, clusters, DEPTH, size), jnp.bfloat16),
        jax.ShapeDtypeStruct((count, clusters, size), jnp.float32),
        jax.ShapeDtypeStruct((counts[1], clusters, size), jnp.float32),
    ]
    out_specs = [
        pl.BlockSpec((1, clusters, size, DEPTH), lambda i: (place_of(i), 0, 0, 0)),
        pl.BlockSpec((1, clusters, DEPTH, size), lambda i: (place_of(i), 0, 0, 0)),
        pl.BlockSpec((1, clusters, size), lambda i: (place_of(i), 0, 0)),
        pl.BlockSpec((1, clusters, size), lambda i: (told[-1], 0, 0)),
    ]
    parts = 4 if told else 3
    held = [] if state is None else list(state[:parts])
    out = pl.pallas_call(
        body,
        grid=(used,),
        out_shape=shapes[:parts],
        in_specs=[pl.BlockSpec(points.shape, lambda i: (0, 0)) for points, _ in blocks]
        + [pl.BlockSpec(memory_space=pl.ANY)] * (len(held) + len(after)),
        out_specs=out_specs[:parts],
        input_output_aliases={used + i: i for i in range(len(held))},
        compiler_params=pltpu.CompilerParams(vmem_limit_bytes=VMEM),
        cost_estimate=pl.CostEstimate(
            flops=used * clusters * dims * size * 4, bytes_accessed=used * clusters * size * DEPTH * 8, transcendentals=0
        ),
        name="prepare",
    )(*[points for points, _ in blocks], *held, *after)
    return list(out) + ([] if told else [state[3]])


def list_pairs(home, cand, target_bits, tgt_count, early, late):
    sources, per_cluster = cand.shape
    targets = tgt_count << len(target_bits)
    mask = sum(1 << b for b in target_bits)
    nobody = sources * (2 * targets) + targets

    def body(home_ref, cand_ref, out_ref, table_ref, entries_ref, sem):
        code = cand_ref[...]
        apart = lax.div(code, tgt_count) ^ home_ref[2]
        block = sum(((apart >> bit) & 1) << place for place, bit in enumerate(target_bits))
        inside = (apart & ~mask) == 0
        row = lax.broadcasted_iota(jnp.int32, code.shape, 0)
        code = (row ^ (home_ref[0] * tgt_count)) * (2 * targets) + block * tgt_count + lax.rem(code, tgt_count)
        lane = lax.broadcasted_iota(jnp.int32, table_ref.shape, 1)
        table = jnp.full(table_ref.shape, -1, jnp.int32)
        for at in early + late:
            column = jnp.max(jnp.where(inside & (block == at), code, -1), axis=1, keepdims=True)
            table = jnp.where(lane == at, column, table)
        table_ref[...] = table
        copy = pltpu.make_async_copy(table_ref, entries_ref, sem)
        copy.start()
        copy.wait()

        def fill(columns, filled):
            def one(r, filled):
                for u in range(8):
                    for k in columns:
                        entry = entries_ref[r * 8 + u, k]
                        out_ref[filled] = entry
                        filled = filled + jnp.where(entry >= 0, 1, 0).astype(jnp.int32)
                return filled

            return lax.fori_loop(0, sources // 8, one, filled)

        filled = fill(early, jnp.int32(2))
        for extra in range(PART):
            out_ref[filled + extra] = nobody
        begin = lax.div(filled - 2 + (PART - 1), PART) * PART
        filled = fill(late, begin + 2)
        for extra in range(GROUP):
            out_ref[filled + extra] = nobody
        out_ref[0] = begin
        out_ref[1] = filled - 2

    return pl.pallas_call(
        body,
        out_shape=jax.ShapeDtypeStruct((sources * per_cluster + 2 + PART + GROUP,), jnp.int32),
        in_specs=[pl.BlockSpec(memory_space=pltpu.SMEM), pl.BlockSpec(memory_space=pltpu.VMEM)],
        out_specs=pl.BlockSpec(memory_space=pltpu.SMEM),
        scratch_shapes=[
            pltpu.VMEM((sources, 128), jnp.int32), pltpu.SMEM((sources, 128), jnp.int32), pltpu.SemaphoreType.DMA,
        ],
        compiler_params=pltpu.CompilerParams(vmem_limit_bytes=SMALL),
        cost_estimate=pl.CostEstimate(flops=0, bytes_accessed=4 << 20, transcendentals=0),
        name="list_pairs",
    )(home, cand)


def padded_rows(rows):
    return -(-3 * rows // 128) * 128


def sum_pairs(pairs_ref, lhs_ref, rhs_ref, sources, values, extra_ref, acc_ref, by_source, part=ALL, adjust=lambda term: term):
    size = lhs_ref.shape[1]
    targets = lhs_ref.shape[0] - sources
    count, others = (targets, sources) if by_source else (sources, targets)
    lhs_base, rhs_base = (sources, 0) if by_source else (0, sources)
    wide = extra_ref.shape[1]
    parts = list(split3(values))
    if wide > 3 * count:
        parts.append(jnp.zeros((wide - 3 * count, size), jnp.float32))
    extra_ref[...] = jnp.concatenate(parts, axis=0).T.astype(jnp.bfloat16)
    acc_ref[...] = jnp.zeros_like(acc_ref)
    row = lax.broadcasted_iota(jnp.int32, (wide, size), 0)
    row = jnp.where(row < 3 * count, lax.rem(row, count), count)

    length = GROUP if part == ALL else PART

    def step(g, carry):
        for u in range(length):
            code = pairs_ref[g * length + u + 2]
            s, t = lax.div(code, 2 * targets), lax.rem(code, 2 * targets)
            m, place = (t, s) if by_source else (s, t)
            m, n = jnp.minimum(m, count - 1), jnp.minimum(place, others - 1)
            chosen = jnp.where(row == m, 1.0, 0.0).astype(jnp.bfloat16)
            term = jnp.dot(
                jnp.concatenate([lhs_ref[lhs_base + m], extra_ref[...]], axis=1),
                jnp.concatenate([rhs_ref[rhs_base + n], chosen], axis=0),
                preferred_element_type=jnp.float32,
            )
            acc_ref[place] += jnp.sum(jnp.exp(adjust(term)).reshape(size // 8, 8, size), axis=0)
        return carry

    first = lax.div(pairs_ref[0], length) if part == LATE else 0
    stop = lax.div(pairs_ref[0 if part == EARLY else 1] + (length - 1), length)
    lax.fori_loop(first, stop, step, 0)
    return jnp.sum(acc_ref[:others], axis=1)


def moved(block, home, rows):
    return pl.ds(pl.multiple_of((block ^ home) * rows, rows), rows)


def store_sums(sums, home, out_ref, far):
    rows = far.shape[0]
    for block in range(sums.shape[0] // rows):
        part = sums[block * rows:(block + 1) * rows]
        out_ref[moved(block, home, rows), :] = part + far if block == 0 else part


def load_sums(sums_refs, home, rows):
    blocks = []
    for block in range(sums_refs[0].shape[-2] // rows):
        blocks.append(sum(ref[moved(block, home, rows), :] for ref in sums_refs))
    return jnp.concatenate(blocks, axis=0)


def first_row_kernel(sources, known, pairs_ref, home_ref, lhs_ref, rhs_ref, half_ref, far_ref, pot_ref, *refs):
    before_ref, (out_ref, extra_ref, acc_ref) = refs[:-3], refs[-3:]
    pot, half = pot_ref[...], half_ref[sources:, :]
    if known is not None:
        row = lax.broadcasted_iota(jnp.int32, pot.shape, 0)
        is_known = functools.reduce(jnp.logical_or, [(row >= a) & (row < b) for a, b in known])
        pot, half = jnp.where(is_known, pot, 0.0), jnp.where(is_known, half, 0.0)
    values = INV_EPS * (pot - half) - LOW_OFFSET
    run = functools.partial(
        sum_pairs, pairs_ref, lhs_ref, rhs_ref, sources, values, extra_ref, acc_ref, True, LATE if before_ref else EARLY
    )
    far = jnp.exp(far_ref[...] - LOW_OFFSET)
    own = far_ref.shape[0]

    def store(low, high):
        if not before_ref:
            out_ref[0] = low
            out_ref[1] = jnp.zeros_like(low) if high is None else high
            return
        low = low + before_ref[0][0]
        high = before_ref[0][1] if high is None else high + before_ref[0][1]
        low = jnp.concatenate([low[:own] + far, low[own:]], axis=0)
        low, high = log_or_nothing(low) + LOW_OFFSET, log_or_nothing(high) + HIGH_OFFSET
        top = jnp.maximum(low, high)
        logs = top + jnp.log(jnp.exp(low - top) + jnp.exp(high - top))
        store_sums(logs, home_ref[0], out_ref, jnp.zeros_like(far))

    narrow = jnp.max(pot) <= LOW_TOP * SCALE_EPS

    @pl.when(narrow)
    def _():
        store(run(), None)

    @pl.when(jnp.logical_not(narrow))
    def _():
        edge = LOW_TOP - LOW_OFFSET
        low = run(lambda term: jnp.where(term <= edge, term, NOTHING))
        store(low, run(lambda term: jnp.where(term > edge, term - (HIGH_OFFSET - LOW_OFFSET), NOTHING)))


def row_kernel(terms, sources, pairs_ref, home_ref, lhs_ref, rhs_ref, half_ref, far_ref, sums_ref, come_ref, out_ref, extra_ref, acc_ref):
    sums = load_sums([sums_ref, come_ref], home_ref[1], far_ref.shape[0])
    pot = -KEEP_TAU * SCALE_EPS * (jnp.log(sums) - column_offset(terms))
    values = INV_EPS * (pot - half_ref[sources:, :]) - LOW_OFFSET
    total = sum_pairs(pairs_ref, lhs_ref, rhs_ref, sources, values, extra_ref, acc_ref, True)
    store_sums(total, home_ref[0], out_ref, jnp.exp(far_ref[...] - LOW_OFFSET))


def log_or_nothing(value):
    return jnp.where(value > 0.0, jnp.log(jnp.where(value > 0.0, value, 1.0)), NOTHING)


def column_offset(terms):
    return LOG_LARGEST - COLUMN_TOP - math.log(terms)


def column_kernel(terms, sources, first, pairs_ref, home_ref, lhs_ref, rhs_ref, half_ref, far_ref, sums_ref, out_ref, *refs):
    pot_refs, (extra_ref, acc_ref) = refs[:-2], refs[-2:]
    parts, own = range(sums_ref.shape[0]), far_ref.shape[0]
    if first:
        logs = [load_sums([sums_ref.at[i]], home_ref[0], own) for i in parts]
        top = functools.reduce(jnp.maximum, logs)
        log_sum = top + jnp.log(sum(jnp.exp(log - top) for log in logs))
    else:
        log_sum = jnp.log(load_sums([sums_ref.at[i] for i in parts], home_ref[0], own)) + LOW_OFFSET
    pot = -KEEP_TAU * SCALE_EPS * log_sum
    values = INV_EPS * (pot - half_ref[:sources, :]) + column_offset(terms)
    total = sum_pairs(pairs_ref, lhs_ref, rhs_ref, sources, values, extra_ref, acc_ref, False)
    store_sums(total, home_ref[1], out_ref, jnp.exp(far_ref[...] + column_offset(terms)))
    for pot_ref in pot_refs:
        pot_ref[...] = pot[:own]


def run_pass(kernel, out_shapes, pairs, home, state, width, others, tiles, *rest):
    size = state[0].shape[1]
    space = pl.BlockSpec(memory_space=pltpu.VMEM)
    return pl.pallas_call(
        kernel,
        out_shape=out_shapes,
        in_specs=[pl.BlockSpec(memory_space=pltpu.SMEM)] * 2 + [space] * (3 + len(rest)),
        out_specs=jax.tree.map(lambda _: space, out_shapes),
        scratch_shapes=[
            pltpu.VMEM((size, padded_rows(width)), jnp.bfloat16),
            pltpu.VMEM((others + 1, 8, size), jnp.float32),
        ],
        compiler_params=pltpu.CompilerParams(vmem_limit_bytes=VMEM),
        cost_estimate=pl.CostEstimate(
            flops=2 * tiles * size * size * DEPTH, bytes_accessed=8 << 20, transcendentals=tiles * size * size
        ),
        name="tiles",
    )(pairs, home, *state, *rest)


def per_device(src_points, tgt_points, g_init, far_src, far_tgt, cand_owner, cand_local):
    src_count, _, size = src_points.shape
    tgt_count = tgt_points.shape[0]
    per_cluster = cand_owner.shape[1]
    shards = lax.axis_size("src")
    bits = shards.bit_length() - 1
    upper = max(bits // 2 - 1, 0)
    source_bits = [0] + [b for b in range(bits - upper, bits)]
    target_bits = [b for b in range(1, bits - upper)]
    nr, nc = 1 << len(source_bits), 1 << len(target_bits)
    capacity = max(2, min(src_count // 2, 2 * src_count * per_cluster // shards))
    terms = shards * capacity * size

    def across(array, *which):
        apart = sum(1 << bit for bit in which)
        return lax.ppermute(array, "src", [(i, i ^ apart) for i in range(shards)])

    def doubled(array, which):
        blocks = {0: array}
        for place, bit in reversed(list(enumerate(which))):
            blocks.update({at | 1 << place: across(block, bit) for at, block in list(blocks.items())})
        return [blocks[at] for at in range(1 << len(which))]

    def groups(which):
        masks = [sum(1 << bit for place, bit in enumerate(which) if i >> place & 1) for i in range(1 << len(which))]
        return [[base | m for m in masks] for base in range(shards) if not base & sum(1 << b for b in which)]

    def place_of(device, which):
        return sum(((device >> bit) & 1) << place for place, bit in enumerate(which))

    sources, targets = nr * src_count, nc * tgt_count
    dims = src_points.shape[1]
    me = lax.axis_index("src").astype(jnp.int32)
    home = jnp.stack([place_of(me, source_bits), place_of(me, target_bits), me])
    src_points = src_points.reshape(-1, size)
    tgt_message, = pack((tgt_points,), (g_init,))
    late = [at for at in range(2, nc) if at & 1]
    early = [at for at in range(nc) if at not in late]
    ready = functools.partial(prepare, clusters=src_count, dims=dims, counts=(nr, nc))

    src_far = doubled(src_points, source_bits[1:])
    src_side = across(src_points, source_bits[0])
    tgt_far = doubled(tgt_message, target_bits[1:])
    held, home = lax.optimization_barrier((src_points, home))
    state = ready([(held, 0), (tgt_message, nr)], state=None)
    code = cand_owner * tgt_count + cand_local
    code, state, tgt_held = lax.optimization_barrier((code, state, tgt_message))
    tgt_side = across(tgt_held, target_bits[0])
    cand = lax.all_gather(code, "src", axis_index_groups=groups(source_bits)).reshape(sources, per_cluster)
    pairs = list_pairs(home, cand, target_bits, tgt_count, early, late)
    src_far[1:], cand = lax.optimization_barrier((src_far[1:], cand))

    def interleaved(far, side, bit):
        return [b for pair in zip(far, [side] + [across(block, bit) for block in far[1:]]) for b in pair]

    src_blocks = interleaved(src_far, src_side, source_bits[0])
    tgt_blocks = interleaved(tgt_far, tgt_side, target_bits[0])

    def pairs_of(sources_at, targets_at):
        return [(src_blocks[at], at) for at in sources_at] + [(tgt_blocks[at], nr + at) for at in targets_at]

    by_hops = lambda places: sorted(places, key=lambda at: (at.bit_count(), at))[1:]
    src_order, tgt_order = by_hops(range(nr)), by_hops(early)
    for i in range(max(len(src_order), len(tgt_order))):
        state = ready(pairs_of(src_order[i:i + 1], tgt_order[i:i + 1]), state=state)

    def flat(state):
        return [a.reshape((-1,) + a.shape[2:]) for a in state]

    f32 = jnp.float32
    tiles = src_count * per_cluster
    for iteration in range(ITERS):
        first = iteration == 0
        if first:
            known = [(at * tgt_count, (at + 1) * tgt_count) for at in early]
            *operands, pot = flat(state)
            before = run_pass(
                functools.partial(first_row_kernel, sources, known),
                jax.ShapeDtypeStruct((2, sources, size), f32),
                pairs, home, operands, targets, sources, tiles, far_src, pot,
            )
            for at in late:
                state = ready(pairs_of([], [at]), state=state, after=(before,))
            *state, pot = flat(state)
            sums = run_pass(
                functools.partial(first_row_kernel, sources, None),
                jax.ShapeDtypeStruct((sources, size), f32),
                pairs, home, state, targets, sources, tiles, far_src, pot, before,
            )
        else:
            sums = run_pass(
                functools.partial(row_kernel, terms, sources),
                jax.ShapeDtypeStruct((sources, size), f32),
                pairs, home, state, targets, sources, tiles, far_src, *sums,
            )
        sums = lax.all_gather(sums, "src", axis_index_groups=groups(source_bits))
        shapes = [jax.ShapeDtypeStruct((targets, size), f32), jax.ShapeDtypeStruct((src_count, size), f32)]
        column, *src_pot = run_pass(
            functools.partial(column_kernel, terms, sources, first),
            shapes if iteration + 1 == ITERS else shapes[:1],
            pairs, home, state, sources, targets, tiles, far_tgt, sums,
        )
        if iteration + 1 < ITERS:
            for bit in target_bits[:-1]:
                column = column + across(column, bit)
            sums = [column, across(column, target_bits[-1])]
    column = lax.all_to_all(
        column.reshape(nc, tgt_count, size), "src", 0, 0, tiled=True, axis_index_groups=groups(target_bits)
    )
    tgt_pot = -KEEP_TAU * SCALE_EPS * (jnp.log(jnp.sum(column, axis=0)) - column_offset(terms))
    return (src_pot[0], tgt_pot)


def solution(mesh):
    return jax.shard_map(
        per_device,
        mesh=mesh,
        in_specs=(
            P(("groups", "src"), None, None),
            P(("groups", "src"), None, None),
            P(("groups", "src"), None),
            P(("groups", "src"), None),
            P(("groups", "src"), None),
            P(("groups", "src"), None),
            P(("groups", "src"), None),
        ),
        out_specs=(P(("groups", "src"), None), P(("groups", "src"), None)),
        check_vma=False,
    )
```

```python
import functools
import math

import jax
import jax.numpy as jnp
from jax import lax
from jax.experimental import pallas as pl
from jax.experimental.pallas import tpu as pltpu
from jax.sharding import PartitionSpec as P

ITERS = 2
SCALE_EPS = 0.25
KEEP_TAU = 0.8
INV_EPS = 1.0 / SCALE_EPS

LOW_OFFSET = 60.0
LOW_TOP = 130.0
HIGH_OFFSET = 200.0
COLUMN_TOP = -KEEP_TAU * 10.0
LOG_LARGEST = 88.4

NOTHING = -1e30
ALL, EARLY, LATE = range(3)

DEPTH = 128
GROUP = 64
PART = 16
EXTRA = 32
VMEM = 12 * 1024 * 1024
SMALL = 1024 * 1024
LARGE = 60 * 1024 * 1024


def split3(value):
    high = value.astype(jnp.bfloat16).astype(jnp.float32)
    rest = value - high
    mid = rest.astype(jnp.bfloat16).astype(jnp.float32)
    return high, mid, rest - mid


def pack(points, *rows):
    clusters, dims, size = points[0].shape
    counts = [len(r) for r in rows]
    tall = clusters * dims

    flat = [p.reshape(tall, size) for p in points]
    few = [r for r in rows for r in r]

    def body(*refs):
        points_refs, refs = refs[:len(points)], refs[len(points):]
        few_refs, refs = refs[:len(few)], refs[len(few):]
        out_refs, refs = refs[:len(points)], refs[len(points):]
        held_refs, sems = refs[:-1], refs[-1]
        copies = [pltpu.make_async_copy(p, o.at[:tall], sems.at[i]) for i, (p, o) in enumerate(zip(points_refs, out_refs))]
        loads = [pltpu.make_async_copy(f, h, sems.at[len(copies) + i]) for i, (f, h) in enumerate(zip(few_refs, held_refs))]
        for copy in loads + copies:
            copy.start()
        for copy in loads:
            copy.wait()
        held = list(held_refs)
        for i, n in enumerate(counts):
            mine, held = held[:n], held[n:]
            if n > 1:
                values = [ref[...].astype(jnp.float32) for ref in mine]
                values = [jnp.concatenate([v, jnp.zeros((v.shape[0], size - v.shape[1]), jnp.float32)], axis=1) for v in values]
            else:
                values = list(split3(mine[0][...]))
            empty = EXTRA - sum(v.shape[0] for v in values)
            if empty:
                values.append(jnp.zeros((empty, size), jnp.float32))
            out_refs[i][tall:, :] = jnp.concatenate(values, axis=0).astype(jnp.bfloat16)
        for copy in copies:
            copy.wait()

    return pl.pallas_call(
        body,
        out_shape=[jax.ShapeDtypeStruct((tall + EXTRA, size), p.dtype) for p in points],
        in_specs=[pl.BlockSpec(memory_space=pltpu.HBM)] * (len(points) + len(few)),
        out_specs=[pl.BlockSpec(memory_space=pltpu.VMEM)] * len(points),
        scratch_shapes=[pltpu.VMEM(f.shape, f.dtype) for f in few] + [pltpu.SemaphoreType.DMA((len(points) + len(few),))],
        compiler_params=pltpu.CompilerParams(vmem_limit_bytes=LARGE),
        name="pack",
    )(*flat, *few)


def prepare(blocks, clusters, dims, counts, state, after=()):
    size = blocks[0][0].shape[1]
    tall = clusters * dims
    places = [place for _, place in blocks]
    used = len(blocks)
    told = [place - counts[0] for place in places if place >= counts[0]]
    latest = []
    for place in places:
        latest.append(place - counts[0] if place >= counts[0] else latest[-1] if latest else told[0] if told else 0)

    def body(*refs):
        points_refs = refs[:used]
        lhs_ref, rhs_ref, half_ref = refs[-4:-1] if told else refs[-3:]
        row = lax.broadcasted_iota(jnp.int32, (DEPTH - dims, size), 0)
        ones = jnp.where(row < 3, 1.0, 0.0).astype(jnp.bfloat16)

        def write(points_ref, place):
            if place >= counts[0]:
                extra = points_ref[tall:, :].astype(jnp.float32)
                refs[-1][0] = extra[:clusters] + extra[clusters:2 * clusters] + extra[2 * clusters:3 * clusters]

            def one(c, carry):
                raw = points_ref[pl.ds(pl.multiple_of(c * dims, dims), dims), :]
                wide = raw.astype(jnp.float32)
                half = 0.5 * jnp.sum(wide * wide, axis=0, keepdims=True)
                half_ref[0, pl.ds(c, 1), :] = half
                high, mid, low = split3(-INV_EPS * half)
                extra = jnp.where(row == 0, high, jnp.where(row == 1, mid, jnp.where(row == 2, low, 0.0)))
                rhs_ref[0, c, :dims, :] = raw
                rhs_ref[0, c, dims:, :] = extra.astype(jnp.bfloat16)
                lhs_ref[0, c] = jnp.concatenate([raw * jnp.asarray(INV_EPS, raw.dtype), ones], axis=0).T
                return carry

            lax.fori_loop(0, clusters, one, 0, unroll=True)

        for i, points_ref in enumerate(points_refs):
            pl.when(pl.program_id(0) == i)(functools.partial(write, points_ref, places[i]))

    def at_step(i, values):
        chosen = values[0]
        for j, value in enumerate(values[1:]):
            chosen = jnp.where(i > j, value, chosen)
        return chosen

    def place_of(i):
        return at_step(i, places)

    count = sum(counts)
    shapes = [
        jax.ShapeDtypeStruct((count, clusters, size, DEPTH), jnp.bfloat16),
        jax.ShapeDtypeStruct((count, clusters, DEPTH, size), jnp.bfloat16),
        jax.ShapeDtypeStruct((count, clusters, size), jnp.float32),
        jax.ShapeDtypeStruct((counts[1], clusters, size), jnp.float32),
    ]
    out_specs = [
        pl.BlockSpec((1, clusters, size, DEPTH), lambda i: (place_of(i), 0, 0, 0)),
        pl.BlockSpec((1, clusters, DEPTH, size), lambda i: (place_of(i), 0, 0, 0)),
        pl.BlockSpec((1, clusters, size), lambda i: (place_of(i), 0, 0)),
        pl.BlockSpec((1, clusters, size), lambda i: (at_step(i, latest), 0, 0)),
    ]
    parts = 4 if told else 3
    held = [] if state is None else list(state[:parts])
    out = pl.pallas_call(
        body,
        grid=(used,),
        out_shape=shapes[:parts],
        in_specs=[pl.BlockSpec(points.shape, lambda i: (0, 0)) for points, _ in blocks]
        + [pl.BlockSpec(memory_space=pl.ANY)] * (len(held) + len(after)),
        out_specs=out_specs[:parts],
        input_output_aliases={used + i: i for i in range(len(held))},
        compiler_params=pltpu.CompilerParams(vmem_limit_bytes=VMEM),
        cost_estimate=pl.CostEstimate(
            flops=used * clusters * dims * size * 4, bytes_accessed=used * clusters * size * DEPTH * 8, transcendentals=0
        ),
        name="prepare",
    )(*[points for points, _ in blocks], *held, *after)
    return list(out) + ([] if told else [state[3]])


def list_pairs(home, cand, target_bits, tgt_count, early, late):
    sources, per_cluster = cand.shape
    targets = tgt_count << len(target_bits)
    mask = sum(1 << b for b in target_bits)
    nobody = sources * (2 * targets) + targets

    def body(home_ref, cand_ref, out_ref, table_ref, entries_ref, sem):
        code = cand_ref[...]
        apart = lax.div(code, tgt_count) ^ home_ref[2]
        block = sum(((apart >> bit) & 1) << place for place, bit in enumerate(target_bits))
        inside = (apart & ~mask) == 0
        row = lax.broadcasted_iota(jnp.int32, code.shape, 0)
        code = (row ^ (home_ref[0] * tgt_count)) * (2 * targets) + block * tgt_count + lax.rem(code, tgt_count)
        lane = lax.broadcasted_iota(jnp.int32, table_ref.shape, 1)
        table = jnp.full(table_ref.shape, -1, jnp.int32)
        for at in early + late:
            column = jnp.max(jnp.where(inside & (block == at), code, -1), axis=1, keepdims=True)
            table = jnp.where(lane == at, column, table)
        table_ref[...] = table
        copy = pltpu.make_async_copy(table_ref, entries_ref, sem)
        copy.start()
        copy.wait()

        def fill(columns, filled):
            def one(r, filled):
                for u in range(8):
                    for k in columns:
                        entry = entries_ref[r * 8 + u, k]
                        out_ref[filled] = entry
                        filled = filled + jnp.where(entry >= 0, 1, 0).astype(jnp.int32)
                return filled

            return lax.fori_loop(0, sources // 8, one, filled)

        filled = fill(early, jnp.int32(2))

        @pl.when(lax.rem(filled - 2, PART) != 0)
        def _():
            for extra in range(PART):
                out_ref[filled + extra] = nobody

        begin = lax.div(filled - 2 + (PART - 1), PART) * PART
        filled = fill(late, begin + 2)

        @pl.when(lax.rem(filled - 2, GROUP) != 0)
        def _():
            for extra in range(GROUP):
                out_ref[filled + extra] = nobody

        out_ref[0] = begin
        out_ref[1] = filled - 2

    return pl.pallas_call(
        body,
        out_shape=jax.ShapeDtypeStruct((sources * per_cluster + 2 + PART + GROUP,), jnp.int32),
        in_specs=[pl.BlockSpec(memory_space=pltpu.SMEM), pl.BlockSpec(memory_space=pltpu.VMEM)],
        out_specs=pl.BlockSpec(memory_space=pltpu.SMEM),
        scratch_shapes=[
            pltpu.VMEM((sources, 128), jnp.int32), pltpu.SMEM((sources, 128), jnp.int32), pltpu.SemaphoreType.DMA,
        ],
        compiler_params=pltpu.CompilerParams(vmem_limit_bytes=SMALL),
        cost_estimate=pl.CostEstimate(flops=0, bytes_accessed=4 << 20, transcendentals=0),
        name="list_pairs",
    )(home, cand)


def padded_rows(rows):
    return -(-3 * rows // 128) * 128


def sum_pairs(pairs_ref, lhs_ref, rhs_ref, sources, values, extra_ref, acc_ref, by_source, part=ALL, adjust=lambda term: term):
    size = lhs_ref.shape[1]
    targets = lhs_ref.shape[0] - sources
    count, others = (targets, sources) if by_source else (sources, targets)
    lhs_base, rhs_base = (sources, 0) if by_source else (0, sources)
    wide = extra_ref.shape[1]
    parts = list(split3(values))
    if wide > 3 * count:
        parts.append(jnp.zeros((wide - 3 * count, size), jnp.float32))
    extra_ref[...] = jnp.concatenate(parts, axis=0).T.astype(jnp.bfloat16)
    acc_ref[...] = jnp.zeros_like(acc_ref)
    row = lax.broadcasted_iota(jnp.int32, (wide, size), 0)
    row = jnp.where(row < 3 * count, lax.rem(row, count), count)

    length = GROUP if part == ALL else PART

    def step(g, carry):
        for u in range(length):
            code = pairs_ref[g * length + u + 2]
            s, t = lax.div(code, 2 * targets), lax.rem(code, 2 * targets)
            m, place = (t, s) if by_source else (s, t)
            m, n = jnp.minimum(m, count - 1), jnp.minimum(place, others - 1)
            chosen = jnp.where(row == m, 1.0, 0.0).astype(jnp.bfloat16)
            term = jnp.dot(
                jnp.concatenate([lhs_ref[lhs_base + m], extra_ref[...]], axis=1),
                jnp.concatenate([rhs_ref[rhs_base + n], chosen], axis=0),
                preferred_element_type=jnp.float32,
            )
            acc_ref[place] += jnp.sum(jnp.exp(adjust(term)).reshape(size // 8, 8, size), axis=0)
        return carry

    first = lax.div(pairs_ref[0], length) if part == LATE else 0
    stop = lax.div(pairs_ref[0 if part == EARLY else 1] + (length - 1), length)
    lax.fori_loop(first, stop, step, 0)
    return jnp.sum(acc_ref[:others], axis=1)


def moved(block, home, rows):
    return pl.ds(pl.multiple_of((block ^ home) * rows, rows), rows)


def store_sums(sums, home, out_ref, far):
    rows = far.shape[0]
    for block in range(sums.shape[0] // rows):
        part = sums[block * rows:(block + 1) * rows]
        out_ref[moved(block, home, rows), :] = part + far if block == 0 else part


def load_sums(sums_refs, home, rows):
    blocks = []
    for block in range(sums_refs[0].shape[-2] // rows):
        blocks.append(sum(ref[moved(block, home, rows), :] for ref in sums_refs))
    return jnp.concatenate(blocks, axis=0)


def first_row_kernel(sources, known, pairs_ref, home_ref, lhs_ref, rhs_ref, half_ref, far_ref, pot_ref, *refs):
    before_ref, (out_ref, extra_ref, acc_ref) = refs[:-3], refs[-3:]
    pot, half = pot_ref[...], half_ref[sources:, :]
    if known is not None:
        row = lax.broadcasted_iota(jnp.int32, pot.shape, 0)
        is_known = functools.reduce(jnp.logical_or, [(row >= a) & (row < b) for a, b in known])
        pot, half = jnp.where(is_known, pot, 0.0), jnp.where(is_known, half, 0.0)
    values = INV_EPS * (pot - half) - LOW_OFFSET
    run = functools.partial(
        sum_pairs, pairs_ref, lhs_ref, rhs_ref, sources, values, extra_ref, acc_ref, True, LATE if before_ref else EARLY
    )
    far = jnp.exp(far_ref[...] - LOW_OFFSET)
    own = far_ref.shape[0]

    def store(low, high):
        if not before_ref:
            out_ref[0] = low
            out_ref[1] = jnp.zeros_like(low) if high is None else high
            return
        low = low + before_ref[0][0]
        high = before_ref[0][1] if high is None else high + before_ref[0][1]
        low = jnp.concatenate([low[:own] + far, low[own:]], axis=0)
        low, high = log_or_nothing(low) + LOW_OFFSET, log_or_nothing(high) + HIGH_OFFSET
        top = jnp.maximum(low, high)
        logs = top + jnp.log(jnp.exp(low - top) + jnp.exp(high - top))
        store_sums(logs, home_ref[0], out_ref, jnp.zeros_like(far))

    narrow = jnp.max(pot) <= LOW_TOP * SCALE_EPS

    @pl.when(narrow)
    def _():
        store(run(), None)

    @pl.when(jnp.logical_not(narrow))
    def _():
        edge = LOW_TOP - LOW_OFFSET
        low = run(lambda term: jnp.where(term <= edge, term, NOTHING))
        store(low, run(lambda term: jnp.where(term > edge, term - (HIGH_OFFSET - LOW_OFFSET), NOTHING)))


def row_kernel(terms, sources, pairs_ref, home_ref, lhs_ref, rhs_ref, half_ref, far_ref, sums_ref, out_ref, extra_ref, acc_ref):
    sums = load_sums([sums_ref.at[i] for i in range(sums_ref.shape[0])], home_ref[1], far_ref.shape[0])
    pot = -KEEP_TAU * SCALE_EPS * (jnp.log(sums) - column_offset(terms))
    values = INV_EPS * (pot - half_ref[sources:, :]) - LOW_OFFSET
    total = sum_pairs(pairs_ref, lhs_ref, rhs_ref, sources, values, extra_ref, acc_ref, True)
    store_sums(total, home_ref[0], out_ref, jnp.exp(far_ref[...] - LOW_OFFSET))


def log_or_nothing(value):
    return jnp.where(value > 0.0, jnp.log(jnp.where(value > 0.0, value, 1.0)), NOTHING)


def column_offset(terms):
    return LOG_LARGEST - COLUMN_TOP - math.log(terms)


def column_kernel(terms, sources, first, last, pairs_ref, home_ref, lhs_ref, rhs_ref, half_ref, far_ref, sums_ref, out_ref, *refs):
    pot_refs, (extra_ref, acc_ref, own_ref, sem) = refs[:-4], refs[-4:]
    parts, own = range(sums_ref.shape[0]), far_ref.shape[0]
    if first:
        logs = [load_sums([sums_ref.at[i]], home_ref[0], own) for i in parts]
        top = functools.reduce(jnp.maximum, logs)
        log_sum = top + jnp.log(sum(jnp.exp(log - top) for log in logs))
    else:
        log_sum = jnp.log(load_sums([sums_ref.at[i] for i in parts], home_ref[0], own)) + LOW_OFFSET
    pot = -KEEP_TAU * SCALE_EPS * log_sum
    own_ref[...] = pot[:own]
    copies = [pltpu.make_async_copy(own_ref, pot_ref, sem) for pot_ref in pot_refs]
    for copy in copies:
        copy.start()
    values = INV_EPS * (pot - half_ref[:sources, :]) + column_offset(terms)
    total = sum_pairs(pairs_ref, lhs_ref, rhs_ref, sources, values, extra_ref, acc_ref, False)
    far = jnp.exp(far_ref[...] + column_offset(terms))
    for out_at in [out_ref.at[i] for i in range(out_ref.shape[0])] if not last else [out_ref]:
        store_sums(total, home_ref[1], out_at, far)
    for copy in copies:
        copy.wait()


def run_pass(kernel, out_shapes, pairs, home, state, width, others, tiles, *rest, scratch=()):
    size = state[0].shape[1]
    space = pl.BlockSpec(memory_space=pltpu.VMEM)
    return pl.pallas_call(
        kernel,
        out_shape=out_shapes,
        in_specs=[pl.BlockSpec(memory_space=pltpu.SMEM)] * 2 + [space] * (3 + len(rest)),
        out_specs=[space] + [pl.BlockSpec(memory_space=pl.ANY)] * (len(out_shapes) - 1) if isinstance(out_shapes, list) else space,
        scratch_shapes=[
            pltpu.VMEM((size, padded_rows(width)), jnp.bfloat16),
            pltpu.VMEM((others + 1, 8, size), jnp.float32),
            *scratch,
        ],
        compiler_params=pltpu.CompilerParams(vmem_limit_bytes=VMEM),
        cost_estimate=pl.CostEstimate(
            flops=2 * tiles * size * size * DEPTH, bytes_accessed=8 << 20, transcendentals=tiles * size * size
        ),
        name="tiles",
    )(pairs, home, *state, *rest)


def per_device(src_points, tgt_points, g_init, far_src, far_tgt, cand_owner, cand_local):
    src_count, _, size = src_points.shape
    tgt_count = tgt_points.shape[0]
    per_cluster = cand_owner.shape[1]
    shards = lax.axis_size("src")
    bits = shards.bit_length() - 1
    upper = max(bits // 2 - 1, 0)
    source_bits = [0] + [b for b in range(bits - upper, bits)]
    target_bits = [b for b in range(1, bits - upper)]
    nr, nc = 1 << len(source_bits), 1 << len(target_bits)
    capacity = max(2, min(src_count // 2, 2 * src_count * per_cluster // shards))
    terms = shards * capacity * size

    def across(array, *which):
        apart = sum(1 << bit for bit in which)
        return lax.ppermute(array, "src", [(i, i ^ apart) for i in range(shards)])

    def doubled(array, which):
        blocks = {0: array}
        for place, bit in reversed(list(enumerate(which))):
            blocks.update({at | 1 << place: across(block, bit) for at, block in list(blocks.items())})
        return [blocks[at] for at in range(1 << len(which))]

    def groups(which):
        masks = [sum(1 << bit for place, bit in enumerate(which) if i >> place & 1) for i in range(1 << len(which))]
        return [[base | m for m in masks] for base in range(shards) if not base & sum(1 << b for b in which)]

    def place_of(device, which):
        return sum(((device >> bit) & 1) << place for place, bit in enumerate(which))

    sources, targets = nr * src_count, nc * tgt_count
    dims = src_points.shape[1]
    me = lax.axis_index("src").astype(jnp.int32)
    home = jnp.stack([place_of(me, source_bits), place_of(me, target_bits), me])
    src_points = src_points.reshape(-1, size)
    tgt_message, = pack((tgt_points,), (g_init,))
    late = [at for at in range(2, nc) if at & 1]
    early = [at for at in range(nc) if at not in late]
    ready = functools.partial(prepare, clusters=src_count, dims=dims, counts=(nr, nc))

    src_far = doubled(src_points, source_bits[1:])
    src_side = across(src_points, source_bits[0])
    tgt_far = doubled(tgt_message, target_bits[1:])
    held, home = lax.optimization_barrier((src_points, home))
    state = ready([(held, 0), (tgt_message, nr)], state=None)
    code = cand_owner * tgt_count + cand_local
    code, state, tgt_held = lax.optimization_barrier((code, state, tgt_message))
    tgt_side = across(tgt_held, target_bits[0])
    cand = lax.all_gather(code, "src", axis_index_groups=groups(source_bits)).reshape(sources, per_cluster)
    pairs = list_pairs(home, cand, target_bits, tgt_count, early, late)
    src_far[1:], cand = lax.optimization_barrier((src_far[1:], cand))

    def interleaved(far, side, bit):
        return [b for pair in zip(far, [side] + [across(block, bit) for block in far[1:]]) for b in pair]

    src_blocks = interleaved(src_far, src_side, source_bits[0])
    tgt_blocks = interleaved(tgt_far, tgt_side, target_bits[0])

    def pairs_of(sources_at, targets_at):
        return [(src_blocks[at], at) for at in sources_at] + [(tgt_blocks[at], nr + at) for at in targets_at]

    state = ready(pairs_of([], early[1:2]) + pairs_of(range(1, 2), early[2:]) + pairs_of(range(2, nr), []), state=state)

    def flat(state):
        return [a.reshape((-1,) + a.shape[2:]) for a in state]

    f32 = jnp.float32
    tiles = src_count * per_cluster
    for iteration in range(ITERS):
        first = iteration == 0
        if first:
            known = [(at * tgt_count, (at + 1) * tgt_count) for at in early]
            *operands, pot = flat(state)
            before = run_pass(
                functools.partial(first_row_kernel, sources, known),
                jax.ShapeDtypeStruct((2, sources, size), f32),
                pairs, home, operands, targets, sources, tiles, far_src, pot,
            )
            for at in late:
                state = ready(pairs_of([], [at]), state=state, after=(before,))
            *state, pot = flat(state)
            sums = run_pass(
                functools.partial(first_row_kernel, sources, None),
                jax.ShapeDtypeStruct((sources, size), f32),
                pairs, home, state, targets, sources, tiles, far_src, pot, before,
            )
        else:
            sums = run_pass(
                functools.partial(row_kernel, terms, sources),
                jax.ShapeDtypeStruct((sources, size), f32),
                pairs, home, state, targets, sources, tiles, far_src, sums,
            )
        sums = lax.all_gather(sums, "src", axis_index_groups=groups(source_bits))
        last = iteration + 1 == ITERS
        shapes = [jax.ShapeDtypeStruct((targets, size) if last else (nc, targets, size), f32)]
        shapes += [jax.ShapeDtypeStruct((src_count, size), f32)] if last else []
        column, *src_pot = run_pass(
            functools.partial(column_kernel, terms, sources, first, last),
            shapes,
            pairs, home, state, sources, targets, tiles, far_tgt, sums,
            scratch=(pltpu.VMEM((src_count, size), f32), pltpu.SemaphoreType.DMA),
        )
        if not last:
            sums = lax.all_to_all(column, "src", 0, 0, tiled=True, axis_index_groups=groups(target_bits))
    column = lax.all_to_all(
        column.reshape(nc, tgt_count, size), "src", 0, 0, tiled=True, axis_index_groups=groups(target_bits)
    )
    tgt_pot = -KEEP_TAU * SCALE_EPS * (jnp.log(sum(column[at] for at in range(nc))) - column_offset(terms))
    return (src_pot[0], tgt_pot)


def solution(mesh):
    return jax.shard_map(
        per_device,
        mesh=mesh,
        in_specs=(
            P(("groups", "src"), None, None),
            P(("groups", "src"), None, None),
            P(("groups", "src"), None),
            P(("groups", "src"), None),
            P(("groups", "src"), None),
            P(("groups", "src"), None),
            P(("groups", "src"), None),
        ),
        out_specs=(P(("groups", "src"), None), P(("groups", "src"), None)),
        check_vma=False,
    )
```

```python
import functools
import math

import jax
import jax.numpy as jnp
from jax import lax
from jax.experimental import pallas as pl
from jax.experimental.pallas import tpu as pltpu
from jax.sharding import PartitionSpec as P

ITERS = 2
SCALE_EPS = 0.25
KEEP_TAU = 0.8
INV_EPS = 1.0 / SCALE_EPS

LOW_OFFSET = 60.0
LOW_TOP = 130.0
HIGH_OFFSET = 200.0
COLUMN_TOP = -KEEP_TAU * 10.0
LOG_LARGEST = 88.4

NOTHING = -1e30
ALL, EARLY, LATE = range(3)

DEPTH = 128
GROUP = 64
PART = 16
EXTRA = 32
VMEM = 12 * 1024 * 1024
SMALL = 1024 * 1024
LARGE = 60 * 1024 * 1024


def split3(value):
    high = value.astype(jnp.bfloat16).astype(jnp.float32)
    rest = value - high
    mid = rest.astype(jnp.bfloat16).astype(jnp.float32)
    return high, mid, rest - mid


def pack(points, potentials):
    tall, size = points.shape

    def body(points_ref, potentials_ref, out_ref):
        out_ref[:tall, :] = points_ref[...]
        terms = list(split3(potentials_ref[...]))
        empty = EXTRA - sum(t.shape[0] for t in terms)
        if empty:
            terms.append(jnp.zeros((empty, size), jnp.float32))
        out_ref[tall:, :] = jnp.concatenate(terms, axis=0).astype(jnp.bfloat16)

    space = pl.BlockSpec(memory_space=pltpu.VMEM)
    return pl.pallas_call(
        body,
        out_shape=jax.ShapeDtypeStruct((tall + EXTRA, size), points.dtype),
        in_specs=[space] * 2,
        out_specs=space,
        compiler_params=pltpu.CompilerParams(vmem_limit_bytes=LARGE),
        name="pack",
    )(points, potentials)


def prepare(blocks, clusters, dims, counts, state, after=()):
    size = blocks[0][0].shape[1]
    tall = clusters * dims
    places = [place for _, place in blocks]
    used = len(blocks)
    told = [place - counts[0] for place in places if place >= counts[0]]
    latest = []
    for place in places:
        latest.append(place - counts[0] if place >= counts[0] else latest[-1] if latest else told[0] if told else 0)

    def body(*refs):
        points_refs = refs[:used]
        lhs_ref, rhs_ref, half_ref = refs[-4:-1] if told else refs[-3:]
        row = lax.broadcasted_iota(jnp.int32, (DEPTH - dims, size), 0)
        ones = jnp.where(row < 3, 1.0, 0.0).astype(jnp.bfloat16)

        def write(points_ref, place):
            if place >= counts[0]:
                extra = points_ref[tall:, :].astype(jnp.float32)
                refs[-1][0] = extra[:clusters] + extra[clusters:2 * clusters] + extra[2 * clusters:3 * clusters]

            def one(c, carry):
                raw = points_ref[pl.ds(pl.multiple_of(c * dims, dims), dims), :]
                wide = raw.astype(jnp.float32)
                half = 0.5 * jnp.sum(wide * wide, axis=0, keepdims=True)
                half_ref[0, pl.ds(c, 1), :] = half
                high, mid, low = split3(-INV_EPS * half)
                extra = jnp.where(row == 0, high, jnp.where(row == 1, mid, jnp.where(row == 2, low, 0.0)))
                rhs_ref[0, c, :dims, :] = raw
                rhs_ref[0, c, dims:, :] = extra.astype(jnp.bfloat16)
                lhs_ref[0, c] = jnp.concatenate([raw * jnp.asarray(INV_EPS, raw.dtype), ones], axis=0).T
                return carry

            lax.fori_loop(0, clusters, one, 0, unroll=True)

        for i, points_ref in enumerate(points_refs):
            pl.when(pl.program_id(0) == i)(functools.partial(write, points_ref, places[i]))

    def at_step(i, values):
        chosen = values[0]
        for j, value in enumerate(values[1:]):
            chosen = jnp.where(i > j, value, chosen)
        return chosen

    def place_of(i):
        return at_step(i, places)

    count = sum(counts)
    shapes = [
        jax.ShapeDtypeStruct((count, clusters, size, DEPTH), jnp.bfloat16),
        jax.ShapeDtypeStruct((count, clusters, DEPTH, size), jnp.bfloat16),
        jax.ShapeDtypeStruct((count, clusters, size), jnp.float32),
        jax.ShapeDtypeStruct((counts[1], clusters, size), jnp.float32),
    ]
    out_specs = [
        pl.BlockSpec((1, clusters, size, DEPTH), lambda i: (place_of(i), 0, 0, 0)),
        pl.BlockSpec((1, clusters, DEPTH, size), lambda i: (place_of(i), 0, 0, 0)),
        pl.BlockSpec((1, clusters, size), lambda i: (place_of(i), 0, 0)),
        pl.BlockSpec((1, clusters, size), lambda i: (at_step(i, latest), 0, 0)),
    ]
    parts = 4 if told else 3
    held = [] if state is None else list(state[:parts])
    out = pl.pallas_call(
        body,
        grid=(used,),
        out_shape=shapes[:parts],
        in_specs=[pl.BlockSpec(points.shape, lambda i: (0, 0)) for points, _ in blocks]
        + [pl.BlockSpec(memory_space=pl.ANY)] * (len(held) + len(after)),
        out_specs=out_specs[:parts],
        input_output_aliases={used + i: i for i in range(len(held))},
        compiler_params=pltpu.CompilerParams(vmem_limit_bytes=VMEM),
        cost_estimate=pl.CostEstimate(
            flops=used * clusters * dims * size * 4, bytes_accessed=used * clusters * size * DEPTH * 8, transcendentals=0
        ),
        name="prepare",
    )(*[points for points, _ in blocks], *held, *after)
    return list(out) + ([] if told else [state[3]])


def list_pairs(home, cand, target_bits, tgt_count, early, late):
    sources, per_cluster = cand.shape
    targets = tgt_count << len(target_bits)
    mask = sum(1 << b for b in target_bits)
    nobody = sources * (2 * targets) + targets
    count = len(early) + len(late)
    tall, wide = -(-count // 8) * 8, -(-sources // 128) * 128

    def body(home_ref, cand_ref, out_ref, table_ref, entries_ref, sem):
        code = cand_ref[...].astype(jnp.float32)
        code = jnp.concatenate([code, jnp.zeros((sources, 128 - per_cluster), jnp.float32)], axis=1)
        if wide > sources:
            code = jnp.concatenate([code, jnp.zeros((wide - sources, 128), jnp.float32)], axis=0)
        code = code.T[:per_cluster].astype(jnp.int32)
        apart = lax.div(code, tgt_count) ^ home_ref[2]
        block = sum(((apart >> bit) & 1) << place for place, bit in enumerate(target_bits))
        inside = (apart & ~mask) == 0
        source = lax.broadcasted_iota(jnp.int32, code.shape, 1) ^ (home_ref[0] * tgt_count)
        code = source * (2 * targets) + block * tgt_count + lax.rem(code, tgt_count)
        found = [jnp.max(jnp.where(inside & (block == at), code, -1), axis=0, keepdims=True) for at in range(count)]
        table = jnp.concatenate(found + [jnp.full((tall - count, wide), -1, jnp.int32)] * (tall > count), axis=0)
        table_ref[...] = table
        copy = pltpu.make_async_copy(table_ref, entries_ref, sem)
        copy.start()
        copy.wait()

        def fill(columns, filled):
            def one(r, filled):
                for u in range(8):
                    for k in columns:
                        entry = entries_ref[k, r * 8 + u]
                        out_ref[filled] = entry
                        filled = filled + jnp.where(entry >= 0, 1, 0).astype(jnp.int32)
                return filled

            return lax.fori_loop(0, sources // 8, one, filled)

        filled = fill(early, jnp.int32(2))

        @pl.when(lax.rem(filled - 2, PART) != 0)
        def _():
            for extra in range(PART):
                out_ref[filled + extra] = nobody

        begin = lax.div(filled - 2 + (PART - 1), PART) * PART
        filled = fill(late, begin + 2)

        @pl.when(lax.rem(filled - 2, GROUP) != 0)
        def _():
            for extra in range(GROUP):
                out_ref[filled + extra] = nobody

        out_ref[0] = begin
        out_ref[1] = filled - 2

    return pl.pallas_call(
        body,
        out_shape=jax.ShapeDtypeStruct((sources * per_cluster + 2 + PART + GROUP,), jnp.int32),
        in_specs=[pl.BlockSpec(memory_space=pltpu.SMEM), pl.BlockSpec(memory_space=pltpu.VMEM)],
        out_specs=pl.BlockSpec(memory_space=pltpu.SMEM),
        scratch_shapes=[
            pltpu.VMEM((tall, wide), jnp.int32), pltpu.SMEM((tall, wide), jnp.int32), pltpu.SemaphoreType.DMA,
        ],
        compiler_params=pltpu.CompilerParams(vmem_limit_bytes=SMALL),
        cost_estimate=pl.CostEstimate(flops=0, bytes_accessed=4 << 20, transcendentals=0),
        name="list_pairs",
    )(home, cand)


def padded_rows(rows):
    return -(-3 * rows // 128) * 128


def sum_pairs(pairs_ref, lhs_ref, rhs_ref, sources, values, extra_ref, acc_ref, by_source, part=ALL, adjust=lambda term: term):
    size = lhs_ref.shape[1]
    targets = lhs_ref.shape[0] - sources
    count, others = (targets, sources) if by_source else (sources, targets)
    lhs_base, rhs_base = (sources, 0) if by_source else (0, sources)
    wide = extra_ref.shape[1]
    parts = list(split3(values))
    if wide > 3 * count:
        parts.append(jnp.zeros((wide - 3 * count, size), jnp.float32))
    extra_ref[...] = jnp.concatenate(parts, axis=0).T.astype(jnp.bfloat16)
    acc_ref[...] = jnp.zeros_like(acc_ref)
    row = lax.broadcasted_iota(jnp.int32, (wide, size), 0)
    row = jnp.where(row < 3 * count, lax.rem(row, count), count)

    length = GROUP if part == ALL else PART

    def step(g, carry):
        for u in range(length):
            code = pairs_ref[g * length + u + 2]
            s, t = lax.div(code, 2 * targets), lax.rem(code, 2 * targets)
            m, place = (t, s) if by_source else (s, t)
            m, n = jnp.minimum(m, count - 1), jnp.minimum(place, others - 1)
            chosen = jnp.where(row == m, 1.0, 0.0).astype(jnp.bfloat16)
            term = jnp.dot(
                jnp.concatenate([lhs_ref[lhs_base + m], extra_ref[...]], axis=1),
                jnp.concatenate([rhs_ref[rhs_base + n], chosen], axis=0),
                preferred_element_type=jnp.float32,
            )
            acc_ref[place] += jnp.sum(jnp.exp(adjust(term)).reshape(size // 8, 8, size), axis=0)
        return carry

    first = lax.div(pairs_ref[0], length) if part == LATE else 0
    stop = lax.div(pairs_ref[0 if part == EARLY else 1] + (length - 1), length)
    lax.fori_loop(first, stop, step, 0)
    return jnp.sum(acc_ref[:others], axis=1)


def moved(block, home, rows):
    return pl.ds(pl.multiple_of((block ^ home) * rows, rows), rows)


def store_sums(sums, home, out_ref, far):
    rows = far.shape[0]
    for block in range(sums.shape[0] // rows):
        part = sums[block * rows:(block + 1) * rows]
        out_ref[moved(block, home, rows), :] = part + far if block == 0 else part


def load_sums(sums_refs, home, rows):
    blocks = []
    for block in range(sums_refs[0].shape[-2] // rows):
        blocks.append(sum(ref[moved(block, home, rows), :] for ref in sums_refs))
    return jnp.concatenate(blocks, axis=0)


def first_row_kernel(sources, known, pairs_ref, home_ref, lhs_ref, rhs_ref, half_ref, far_ref, pot_ref, *refs):
    before_ref, (out_ref, extra_ref, acc_ref) = refs[:-3], refs[-3:]
    pot, half = pot_ref[...], half_ref[sources:, :]
    if known is not None:
        row = lax.broadcasted_iota(jnp.int32, pot.shape, 0)
        is_known = functools.reduce(jnp.logical_or, [(row >= a) & (row < b) for a, b in known])
        pot, half = jnp.where(is_known, pot, 0.0), jnp.where(is_known, half, 0.0)
    values = INV_EPS * (pot - half) - LOW_OFFSET
    run = functools.partial(
        sum_pairs, pairs_ref, lhs_ref, rhs_ref, sources, values, extra_ref, acc_ref, True, LATE if before_ref else EARLY
    )
    far = jnp.exp(far_ref[...] - LOW_OFFSET)
    own = far_ref.shape[0]

    def store(low, high):
        if not before_ref:
            out_ref[0] = low
            out_ref[1] = jnp.zeros_like(low) if high is None else high
            return
        low = low + before_ref[0][0]
        high = before_ref[0][1] if high is None else high + before_ref[0][1]
        low = jnp.concatenate([low[:own] + far, low[own:]], axis=0)
        low, high = log_or_nothing(low) + LOW_OFFSET, log_or_nothing(high) + HIGH_OFFSET
        top = jnp.maximum(low, high)
        logs = top + jnp.log(jnp.exp(low - top) + jnp.exp(high - top))
        store_sums(logs, home_ref[0], out_ref, jnp.zeros_like(far))

    narrow = jnp.max(pot) <= LOW_TOP * SCALE_EPS

    @pl.when(narrow)
    def _():
        store(run(), None)

    @pl.when(jnp.logical_not(narrow))
    def _():
        edge = LOW_TOP - LOW_OFFSET
        low = run(lambda term: jnp.where(term <= edge, term, NOTHING))
        store(low, run(lambda term: jnp.where(term > edge, term - (HIGH_OFFSET - LOW_OFFSET), NOTHING)))


def row_kernel(terms, sources, pairs_ref, home_ref, lhs_ref, rhs_ref, half_ref, far_ref, sums_ref, out_ref, extra_ref, acc_ref):
    sums = load_sums([sums_ref.at[i] for i in range(sums_ref.shape[0])], home_ref[1], far_ref.shape[0])
    pot = -KEEP_TAU * SCALE_EPS * (jnp.log(sums) - column_offset(terms))
    values = INV_EPS * (pot - half_ref[sources:, :]) - LOW_OFFSET
    total = sum_pairs(pairs_ref, lhs_ref, rhs_ref, sources, values, extra_ref, acc_ref, True)
    store_sums(total, home_ref[0], out_ref, jnp.exp(far_ref[...] - LOW_OFFSET))


def log_or_nothing(value):
    return jnp.where(value > 0.0, jnp.log(jnp.where(value > 0.0, value, 1.0)), NOTHING)


def column_offset(terms):
    return LOG_LARGEST - COLUMN_TOP - math.log(terms)


def column_kernel(terms, sources, first, last, pairs_ref, home_ref, lhs_ref, rhs_ref, half_ref, far_ref, sums_ref, out_ref, *refs):
    pot_refs, (extra_ref, acc_ref, own_ref, sem) = refs[:-4], refs[-4:]
    parts, own = range(sums_ref.shape[0]), far_ref.shape[0]
    if first:
        logs = [load_sums([sums_ref.at[i]], home_ref[0], own) for i in parts]
        top = functools.reduce(jnp.maximum, logs)
        log_sum = top + jnp.log(sum(jnp.exp(log - top) for log in logs))
    else:
        log_sum = jnp.log(load_sums([sums_ref.at[i] for i in parts], home_ref[0], own)) + LOW_OFFSET
    pot = -KEEP_TAU * SCALE_EPS * log_sum
    own_ref[...] = pot[:own]
    copies = [pltpu.make_async_copy(own_ref, pot_ref, sem) for pot_ref in pot_refs]
    for copy in copies:
        copy.start()
    values = INV_EPS * (pot - half_ref[:sources, :]) + column_offset(terms)
    total = sum_pairs(pairs_ref, lhs_ref, rhs_ref, sources, values, extra_ref, acc_ref, False)
    far = jnp.exp(far_ref[...] + column_offset(terms))
    for out_at in [out_ref.at[i] for i in range(out_ref.shape[0])] if not last else [out_ref]:
        store_sums(total, home_ref[1], out_at, far)
    for copy in copies:
        copy.wait()


def run_pass(kernel, out_shapes, pairs, home, state, width, others, tiles, *rest, scratch=()):
    size = state[0].shape[1]
    space = pl.BlockSpec(memory_space=pltpu.VMEM)
    return pl.pallas_call(
        kernel,
        out_shape=out_shapes,
        in_specs=[pl.BlockSpec(memory_space=pltpu.SMEM)] * 2 + [space] * (3 + len(rest)),
        out_specs=[space] + [pl.BlockSpec(memory_space=pl.ANY)] * (len(out_shapes) - 1) if isinstance(out_shapes, list) else space,
        scratch_shapes=[
            pltpu.VMEM((size, padded_rows(width)), jnp.bfloat16),
            pltpu.VMEM((others + 1, 8, size), jnp.float32),
            *scratch,
        ],
        compiler_params=pltpu.CompilerParams(vmem_limit_bytes=VMEM),
        cost_estimate=pl.CostEstimate(
            flops=2 * tiles * size * size * DEPTH, bytes_accessed=8 << 20, transcendentals=tiles * size * size
        ),
        name="tiles",
    )(pairs, home, *state, *rest)


def per_device(src_points, tgt_points, g_init, far_src, far_tgt, cand_owner, cand_local):
    src_count, _, size = src_points.shape
    tgt_count = tgt_points.shape[0]
    per_cluster = cand_owner.shape[1]
    shards = lax.axis_size("src")
    bits = shards.bit_length() - 1
    upper = max(bits // 2 - 1, 0)
    source_bits = [0] + [b for b in range(bits - upper, bits)]
    target_bits = [b for b in range(1, bits - upper)]
    nr, nc = 1 << len(source_bits), 1 << len(target_bits)
    capacity = max(2, min(src_count // 2, 2 * src_count * per_cluster // shards))
    terms = shards * capacity * size

    def across(array, *which):
        apart = sum(1 << bit for bit in which)
        return lax.ppermute(array, "src", [(i, i ^ apart) for i in range(shards)])

    def doubled(array, which):
        blocks = {0: array}
        for place, bit in reversed(list(enumerate(which))):
            blocks.update({at | 1 << place: across(block, bit) for at, block in list(blocks.items())})
        return [blocks[at] for at in range(1 << len(which))]

    def groups(which):
        masks = [sum(1 << bit for place, bit in enumerate(which) if i >> place & 1) for i in range(1 << len(which))]
        return [[base | m for m in masks] for base in range(shards) if not base & sum(1 << b for b in which)]

    def place_of(device, which):
        return sum(((device >> bit) & 1) << place for place, bit in enumerate(which))

    sources, targets = nr * src_count, nc * tgt_count
    dims = src_points.shape[1]
    me = lax.axis_index("src").astype(jnp.int32)
    home = jnp.stack([place_of(me, source_bits), place_of(me, target_bits), me])
    src_points = src_points.reshape(-1, size)
    tgt_message = pack(tgt_points.reshape(-1, size), g_init)
    late = [at for at in range(2, nc) if at & 1]
    early = [at for at in range(nc) if at not in late]
    ready = functools.partial(prepare, clusters=src_count, dims=dims, counts=(nr, nc))

    src_far = doubled(src_points, source_bits[1:])
    src_side = across(src_points, source_bits[0])
    tgt_far = doubled(tgt_message, target_bits[1:])
    held, home = lax.optimization_barrier((src_points, home))
    state = ready([(held, 0), (tgt_message, nr)], state=None)
    code = cand_owner * tgt_count + cand_local
    code, state, tgt_held = lax.optimization_barrier((code, state, tgt_message))
    tgt_side = across(tgt_held, target_bits[0])
    cand = lax.all_gather(code, "src", axis_index_groups=groups(source_bits)).reshape(sources, per_cluster)
    pairs = list_pairs(home, cand, target_bits, tgt_count, early, late)
    src_far[1:], cand = lax.optimization_barrier((src_far[1:], cand))

    def interleaved(far, side, bit):
        return [b for pair in zip(far, [side] + [across(block, bit) for block in far[1:]]) for b in pair]

    src_blocks = interleaved(src_far, src_side, source_bits[0])
    tgt_blocks = interleaved(tgt_far, tgt_side, target_bits[0])

    def pairs_of(sources_at, targets_at):
        return [(src_blocks[at], at) for at in sources_at] + [(tgt_blocks[at], nr + at) for at in targets_at]

    state = ready(pairs_of([], early[1:2]) + pairs_of(range(1, 2), early[2:]) + pairs_of(range(2, nr), []), state=state)

    def flat(state):
        return [a.reshape((-1,) + a.shape[2:]) for a in state]

    f32 = jnp.float32
    tiles = src_count * per_cluster
    for iteration in range(ITERS):
        first = iteration == 0
        if first:
            known = [(at * tgt_count, (at + 1) * tgt_count) for at in early]
            *operands, pot = flat(state)
            before = run_pass(
                functools.partial(first_row_kernel, sources, known),
                jax.ShapeDtypeStruct((2, sources, size), f32),
                pairs, home, operands, targets, sources, tiles, far_src, pot,
            )
            for at in late:
                state = ready(pairs_of([], [at]), state=state, after=(before,))
            *state, pot = flat(state)
            sums = run_pass(
                functools.partial(first_row_kernel, sources, None),
                jax.ShapeDtypeStruct((sources, size), f32),
                pairs, home, state, targets, sources, tiles, far_src, pot, before,
            )
        else:
            sums = run_pass(
                functools.partial(row_kernel, terms, sources),
                jax.ShapeDtypeStruct((sources, size), f32),
                pairs, home, state, targets, sources, tiles, far_src, sums,
            )
        sums = lax.all_gather(sums, "src", axis_index_groups=groups(source_bits))
        last = iteration + 1 == ITERS
        shapes = [jax.ShapeDtypeStruct((targets, size) if last else (nc, targets, size), f32)]
        shapes += [jax.ShapeDtypeStruct((src_count, size), f32)] if last else []
        column, *src_pot = run_pass(
            functools.partial(column_kernel, terms, sources, first, last),
            shapes,
            pairs, home, state, sources, targets, tiles, far_tgt, sums,
            scratch=(pltpu.VMEM((src_count, size), f32), pltpu.SemaphoreType.DMA),
        )
        if not last:
            sums = lax.all_to_all(column, "src", 0, 0, tiled=True, axis_index_groups=groups(target_bits))
    column = lax.all_to_all(
        column.reshape(nc, tgt_count, size), "src", 0, 0, tiled=True, axis_index_groups=groups(target_bits)
    )
    tgt_pot = -KEEP_TAU * SCALE_EPS * (jnp.log(sum(column[at] for at in range(nc))) - column_offset(terms))
    return (src_pot[0], tgt_pot)


def solution(mesh):
    return jax.shard_map(
        per_device,
        mesh=mesh,
        in_specs=(
            P(("groups", "src"), None, None),
            P(("groups", "src"), None, None),
            P(("groups", "src"), None),
            P(("groups", "src"), None),
            P(("groups", "src"), None),
            P(("groups", "src"), None),
            P(("groups", "src"), None),
        ),
        out_specs=(P(("groups", "src"), None), P(("groups", "src"), None)),
        check_vma=False,
    )
```

```python
import functools
import math

import jax
import jax.numpy as jnp
from jax import lax
from jax.experimental import pallas as pl
from jax.experimental.pallas import tpu as pltpu
from jax.sharding import PartitionSpec as P

ITERS = 2
SCALE_EPS = 0.25
KEEP_TAU = 0.8
INV_EPS = 1.0 / SCALE_EPS

LOW_OFFSET = 60.0
LOW_TOP = 130.0
HIGH_OFFSET = 200.0
COLUMN_TOP = -KEEP_TAU * 10.0
LOG_LARGEST = 88.4

NOTHING = -1e30
ALL, EARLY, LATE = range(3)

DEPTH = 128
GROUP = 64
PART = 16
FIRST = 48
HEAD = 4
EXTRA = 32
VMEM = 12 * 1024 * 1024
SMALL = 1024 * 1024
LARGE = 60 * 1024 * 1024


def split3(value):
    high = value.astype(jnp.bfloat16).astype(jnp.float32)
    rest = value - high
    mid = rest.astype(jnp.bfloat16).astype(jnp.float32)
    return high, mid, rest - mid


def pack(points, potentials):
    tall, size = points.shape

    def body(points_ref, potentials_ref, out_ref):
        out_ref[:tall, :] = points_ref[...]
        terms = list(split3(potentials_ref[...]))
        empty = EXTRA - sum(t.shape[0] for t in terms)
        if empty:
            terms.append(jnp.zeros((empty, size), jnp.float32))
        out_ref[tall:, :] = jnp.concatenate(terms, axis=0).astype(jnp.bfloat16)

    space = pl.BlockSpec(memory_space=pltpu.VMEM)
    return pl.pallas_call(
        body,
        out_shape=jax.ShapeDtypeStruct((tall + EXTRA, size), points.dtype),
        in_specs=[space] * 2,
        out_specs=space,
        compiler_params=pltpu.CompilerParams(vmem_limit_bytes=LARGE),
        name="pack",
    )(points, potentials)


def prepare(blocks, clusters, dims, counts, state, after=()):
    size = blocks[0][0].shape[1]
    tall = clusters * dims
    places = [place for _, place in blocks]
    used = len(blocks)
    told = [place - counts[0] for place in places if place >= counts[0]]
    latest = []
    for place in places:
        latest.append(place - counts[0] if place >= counts[0] else latest[-1] if latest else told[0] if told else 0)

    def body(*refs):
        points_refs = refs[:used]
        lhs_ref, rhs_ref, half_ref = refs[-4:-1] if told else refs[-3:]
        row = lax.broadcasted_iota(jnp.int32, (DEPTH - dims, size), 0)
        ones = jnp.where(row < 3, 1.0, 0.0).astype(jnp.bfloat16)

        def write(points_ref, place):
            if place >= counts[0]:
                extra = points_ref[tall:, :].astype(jnp.float32)
                refs[-1][0] = extra[:clusters] + extra[clusters:2 * clusters] + extra[2 * clusters:3 * clusters]

            def one(c, carry):
                raw = points_ref[pl.ds(pl.multiple_of(c * dims, dims), dims), :]
                wide = raw.astype(jnp.float32)
                half = 0.5 * jnp.sum(wide * wide, axis=0, keepdims=True)
                half_ref[0, pl.ds(c, 1), :] = half
                high, mid, low = split3(-INV_EPS * half)
                extra = jnp.where(row == 0, high, jnp.where(row == 1, mid, jnp.where(row == 2, low, 0.0)))
                rhs_ref[0, c, :dims, :] = raw
                rhs_ref[0, c, dims:, :] = extra.astype(jnp.bfloat16)
                lhs_ref[0, c] = jnp.concatenate([raw * jnp.asarray(INV_EPS, raw.dtype), ones], axis=0).T
                return carry

            lax.fori_loop(0, clusters, one, 0, unroll=True)

        for i, points_ref in enumerate(points_refs):
            pl.when(pl.program_id(0) == i)(functools.partial(write, points_ref, places[i]))

    def at_step(i, values):
        chosen = values[0]
        for j, value in enumerate(values[1:]):
            chosen = jnp.where(i > j, value, chosen)
        return chosen

    def place_of(i):
        return at_step(i, places)

    count = sum(counts)
    shapes = [
        jax.ShapeDtypeStruct((count, clusters, size, DEPTH), jnp.bfloat16),
        jax.ShapeDtypeStruct((count, clusters, DEPTH, size), jnp.bfloat16),
        jax.ShapeDtypeStruct((count, clusters, size), jnp.float32),
        jax.ShapeDtypeStruct((counts[1], clusters, size), jnp.float32),
    ]
    out_specs = [
        pl.BlockSpec((1, clusters, size, DEPTH), lambda i: (place_of(i), 0, 0, 0)),
        pl.BlockSpec((1, clusters, DEPTH, size), lambda i: (place_of(i), 0, 0, 0)),
        pl.BlockSpec((1, clusters, size), lambda i: (place_of(i), 0, 0)),
        pl.BlockSpec((1, clusters, size), lambda i: (at_step(i, latest), 0, 0)),
    ]
    parts = 4 if told else 3
    held = [] if state is None else list(state[:parts])
    out = pl.pallas_call(
        body,
        grid=(used,),
        out_shape=shapes[:parts],
        in_specs=[pl.BlockSpec(points.shape, lambda i: (0, 0)) for points, _ in blocks]
        + [pl.BlockSpec(memory_space=pl.ANY)] * (len(held) + len(after)),
        out_specs=out_specs[:parts],
        input_output_aliases={used + i: i for i in range(len(held))},
        compiler_params=pltpu.CompilerParams(vmem_limit_bytes=VMEM),
        cost_estimate=pl.CostEstimate(
            flops=used * clusters * dims * size * 4, bytes_accessed=used * clusters * size * DEPTH * 8, transcendentals=0
        ),
        name="prepare",
    )(*[points for points, _ in blocks], *held, *after)
    return list(out) + ([] if told else [state[3]])


def list_pairs(home, cand, target_bits, tgt_count, early, late):
    sources, per_cluster = cand.shape
    targets = tgt_count << len(target_bits)
    mask = sum(1 << b for b in target_bits)
    nobody = sources * (2 * targets) + targets
    count = len(early) + len(late)
    tall, wide = -(-count // 8) * 8, -(-sources // 128) * 128

    def body(home_ref, cand_ref, out_ref, table_ref, entries_ref, sem):
        code = cand_ref[...].astype(jnp.float32)
        code = jnp.concatenate([code, jnp.zeros((sources, 128 - per_cluster), jnp.float32)], axis=1)
        if wide > sources:
            code = jnp.concatenate([code, jnp.zeros((wide - sources, 128), jnp.float32)], axis=0)
        code = code.T[:per_cluster].astype(jnp.int32)
        apart = lax.div(code, tgt_count) ^ home_ref[2]
        block = sum(((apart >> bit) & 1) << place for place, bit in enumerate(target_bits))
        inside = (apart & ~mask) == 0
        source = lax.broadcasted_iota(jnp.int32, code.shape, 1) ^ (home_ref[0] * tgt_count)
        code = source * (2 * targets) + block * tgt_count + lax.rem(code, tgt_count)
        found = [jnp.max(jnp.where(inside & (block == at), code, -1), axis=0, keepdims=True) for at in range(count)]
        table = jnp.concatenate(found + [jnp.full((tall - count, wide), -1, jnp.int32)] * (tall > count), axis=0)
        table_ref[...] = table
        copy = pltpu.make_async_copy(table_ref, entries_ref, sem)
        copy.start()
        copy.wait()

        def fill(columns, filled):
            def one(r, filled):
                for u in range(8):
                    for k in columns:
                        entry = entries_ref[k, r * 8 + u]
                        out_ref[filled] = entry
                        filled = filled + jnp.where(entry >= 0, 1, 0).astype(jnp.int32)
                return filled

            return lax.fori_loop(0, sources // 8, one, filled)

        filled = fill(early, jnp.int32(HEAD))

        @pl.when(lax.rem(filled - HEAD, FIRST) != 0)
        def _():
            for extra in range(FIRST):
                out_ref[filled + extra] = nobody

        begin = lax.div(filled - HEAD + (FIRST - 1), FIRST) * FIRST
        filled = fill(late, begin + HEAD)

        @pl.when(lax.rem(filled - HEAD, GROUP) != 0)
        def _():
            for extra in range(GROUP):
                out_ref[filled + extra] = nobody

        out_ref[0] = begin
        out_ref[1] = filled - HEAD
        out_ref[2] = home_ref[0]
        out_ref[3] = home_ref[1]

    return pl.pallas_call(
        body,
        out_shape=jax.ShapeDtypeStruct((sources * per_cluster + HEAD + FIRST + GROUP,), jnp.int32),
        in_specs=[pl.BlockSpec(memory_space=pltpu.SMEM), pl.BlockSpec(memory_space=pltpu.VMEM)],
        out_specs=pl.BlockSpec(memory_space=pltpu.SMEM),
        scratch_shapes=[
            pltpu.VMEM((tall, wide), jnp.int32), pltpu.SMEM((tall, wide), jnp.int32), pltpu.SemaphoreType.DMA,
        ],
        compiler_params=pltpu.CompilerParams(vmem_limit_bytes=SMALL),
        cost_estimate=pl.CostEstimate(flops=0, bytes_accessed=4 << 20, transcendentals=0),
        name="list_pairs",
    )(home, cand)


def padded_rows(rows):
    return -(-3 * rows // 128) * 128


def sum_pairs(pairs_ref, lhs_ref, rhs_ref, sources, values, extra_ref, acc_ref, by_source, part=ALL, adjust=lambda term: term):
    size = lhs_ref.shape[1]
    targets = lhs_ref.shape[0] - sources
    count, others = (targets, sources) if by_source else (sources, targets)
    lhs_base, rhs_base = (sources, 0) if by_source else (0, sources)
    wide = extra_ref.shape[1]
    parts = list(split3(values))
    if wide > 3 * count:
        parts.append(jnp.zeros((wide - 3 * count, size), jnp.float32))
    extra_ref[...] = jnp.concatenate(parts, axis=0).T.astype(jnp.bfloat16)
    acc_ref[...] = jnp.zeros_like(acc_ref)
    row = lax.broadcasted_iota(jnp.int32, (wide, size), 0)
    row = jnp.where(row < 3 * count, lax.rem(row, count), count)

    length = {ALL: GROUP, EARLY: FIRST, LATE: PART}[part]

    def step(g, carry):
        for u in range(length):
            code = pairs_ref[g * length + u + HEAD]
            s, t = lax.div(code, 2 * targets), lax.rem(code, 2 * targets)
            m, place = (t, s) if by_source else (s, t)
            m, n = jnp.minimum(m, count - 1), jnp.minimum(place, others - 1)
            chosen = jnp.where(row == m, 1.0, 0.0).astype(jnp.bfloat16)
            term = jnp.dot(
                jnp.concatenate([lhs_ref[lhs_base + m], extra_ref[...]], axis=1),
                jnp.concatenate([rhs_ref[rhs_base + n], chosen], axis=0),
                preferred_element_type=jnp.float32,
            )
            acc_ref[place] += jnp.sum(jnp.exp(adjust(term)).reshape(size // 8, 8, size), axis=0)
        return carry

    first = lax.div(pairs_ref[0], length) if part == LATE else 0
    stop = lax.div(pairs_ref[0 if part == EARLY else 1] + (length - 1), length)
    lax.fori_loop(first, stop, step, 0)
    return jnp.sum(acc_ref[:others], axis=1)


def moved(block, home, rows):
    return pl.ds(pl.multiple_of((block ^ home) * rows, rows), rows)


def store_sums(sums, home, out_ref, far):
    rows = far.shape[0]
    for block in range(sums.shape[0] // rows):
        part = sums[block * rows:(block + 1) * rows]
        out_ref[moved(block, home, rows), :] = part + far if block == 0 else part


def load_sums(sums_refs, home, rows):
    blocks = []
    for block in range(sums_refs[0].shape[-2] // rows):
        blocks.append(sum(ref[moved(block, home, rows), :] for ref in sums_refs))
    return jnp.concatenate(blocks, axis=0)


def first_row_kernel(sources, known, pairs_ref, lhs_ref, rhs_ref, half_ref, far_ref, pot_ref, *refs):
    before_ref, (out_ref, extra_ref, acc_ref) = refs[:-3], refs[-3:]
    pot, half = pot_ref[...], half_ref[sources:, :]
    if known is not None:
        row = lax.broadcasted_iota(jnp.int32, pot.shape, 0)
        is_known = functools.reduce(jnp.logical_or, [(row >= a) & (row < b) for a, b in known])
        pot, half = jnp.where(is_known, pot, 0.0), jnp.where(is_known, half, 0.0)
    values = INV_EPS * (pot - half) - LOW_OFFSET
    run = functools.partial(
        sum_pairs, pairs_ref, lhs_ref, rhs_ref, sources, values, extra_ref, acc_ref, True, LATE if before_ref else EARLY
    )
    far = jnp.exp(far_ref[...] - LOW_OFFSET)
    own = far_ref.shape[0]

    def store(low, high):
        if not before_ref:
            out_ref[0] = low
            out_ref[1] = jnp.zeros_like(low) if high is None else high
            return
        low = low + before_ref[0][0]
        high = before_ref[0][1] if high is None else high + before_ref[0][1]
        low = jnp.concatenate([low[:own] + far, low[own:]], axis=0)
        low, high = log_or_nothing(low) + LOW_OFFSET, log_or_nothing(high) + HIGH_OFFSET
        top = jnp.maximum(low, high)
        logs = top + jnp.log(jnp.exp(low - top) + jnp.exp(high - top))
        store_sums(logs, pairs_ref[2], out_ref, jnp.zeros_like(far))

    narrow = jnp.max(pot) <= LOW_TOP * SCALE_EPS

    @pl.when(narrow)
    def _():
        store(run(), None)

    @pl.when(jnp.logical_not(narrow))
    def _():
        edge = LOW_TOP - LOW_OFFSET
        low = run(lambda term: jnp.where(term <= edge, term, NOTHING))
        store(low, run(lambda term: jnp.where(term > edge, term - (HIGH_OFFSET - LOW_OFFSET), NOTHING)))


def row_kernel(terms, sources, pairs_ref, lhs_ref, rhs_ref, half_ref, far_ref, sums_ref, out_ref, extra_ref, acc_ref):
    sums = load_sums([sums_ref.at[i] for i in range(sums_ref.shape[0])], pairs_ref[3], far_ref.shape[0])
    pot = -KEEP_TAU * SCALE_EPS * (jnp.log(sums) - column_offset(terms))
    values = INV_EPS * (pot - half_ref[sources:, :]) - LOW_OFFSET
    total = sum_pairs(pairs_ref, lhs_ref, rhs_ref, sources, values, extra_ref, acc_ref, True)
    store_sums(total, pairs_ref[2], out_ref, jnp.exp(far_ref[...] - LOW_OFFSET))


def log_or_nothing(value):
    return jnp.where(value > 0.0, jnp.log(jnp.where(value > 0.0, value, 1.0)), NOTHING)


def column_offset(terms):
    return LOG_LARGEST - COLUMN_TOP - math.log(terms)


def column_kernel(terms, sources, first, last, pairs_ref, lhs_ref, rhs_ref, half_ref, far_ref, sums_ref, out_ref, *refs):
    pot_refs, (extra_ref, acc_ref, own_ref, sem) = refs[:-4], refs[-4:]
    parts, own = range(sums_ref.shape[0]), far_ref.shape[0]
    if first:
        logs = [load_sums([sums_ref.at[i]], pairs_ref[2], own) for i in parts]
        top = functools.reduce(jnp.maximum, logs)
        log_sum = top + jnp.log(sum(jnp.exp(log - top) for log in logs))
    else:
        log_sum = jnp.log(load_sums([sums_ref.at[i] for i in parts], pairs_ref[2], own)) + LOW_OFFSET
    pot = -KEEP_TAU * SCALE_EPS * log_sum
    own_ref[...] = pot[:own]
    copies = [pltpu.make_async_copy(own_ref, pot_ref, sem) for pot_ref in pot_refs]
    for copy in copies:
        copy.start()
    values = INV_EPS * (pot - half_ref[:sources, :]) + column_offset(terms)
    total = sum_pairs(pairs_ref, lhs_ref, rhs_ref, sources, values, extra_ref, acc_ref, False)
    far = jnp.exp(far_ref[...] + column_offset(terms))
    for out_at in [out_ref.at[i] for i in range(out_ref.shape[0])] if not last else [out_ref]:
        store_sums(total, pairs_ref[3], out_at, far)
    for copy in copies:
        copy.wait()


def run_pass(kernel, out_shapes, pairs, state, width, others, tiles, *rest, scratch=()):
    size = state[0].shape[1]
    space = pl.BlockSpec(memory_space=pltpu.VMEM)
    return pl.pallas_call(
        kernel,
        out_shape=out_shapes,
        in_specs=[pl.BlockSpec(memory_space=pltpu.SMEM)] + [space] * (3 + len(rest)),
        out_specs=[space] + [pl.BlockSpec(memory_space=pl.ANY)] * (len(out_shapes) - 1) if isinstance(out_shapes, list) else space,
        scratch_shapes=[
            pltpu.VMEM((size, padded_rows(width)), jnp.bfloat16),
            pltpu.VMEM((others + 1, 8, size), jnp.float32),
            *scratch,
        ],
        compiler_params=pltpu.CompilerParams(vmem_limit_bytes=VMEM),
        cost_estimate=pl.CostEstimate(
            flops=2 * tiles * size * size * DEPTH, bytes_accessed=8 << 20, transcendentals=tiles * size * size
        ),
        name="tiles",
    )(pairs, *state, *rest)


def per_device(src_points, tgt_points, g_init, far_src, far_tgt, cand_owner, cand_local):
    src_count, _, size = src_points.shape
    tgt_count = tgt_points.shape[0]
    per_cluster = cand_owner.shape[1]
    shards = lax.axis_size("src")
    bits = shards.bit_length() - 1
    upper = max(bits // 2 - 1, 0)
    source_bits = [0] + [b for b in range(bits - upper, bits)]
    target_bits = [b for b in range(1, bits - upper)]
    nr, nc = 1 << len(source_bits), 1 << len(target_bits)
    capacity = max(2, min(src_count // 2, 2 * src_count * per_cluster // shards))
    terms = shards * capacity * size

    def across(array, *which):
        apart = sum(1 << bit for bit in which)
        return lax.ppermute(array, "src", [(i, i ^ apart) for i in range(shards)])

    def doubled(array, which):
        blocks = {0: array}
        for place, bit in reversed(list(enumerate(which))):
            blocks.update({at | 1 << place: across(block, bit) for at, block in list(blocks.items())})
        return [blocks[at] for at in range(1 << len(which))]

    def groups(which):
        masks = [sum(1 << bit for place, bit in enumerate(which) if i >> place & 1) for i in range(1 << len(which))]
        return [[base | m for m in masks] for base in range(shards) if not base & sum(1 << b for b in which)]

    def place_of(device, which):
        return sum(((device >> bit) & 1) << place for place, bit in enumerate(which))

    sources, targets = nr * src_count, nc * tgt_count
    dims = src_points.shape[1]
    me = lax.axis_index("src").astype(jnp.int32)
    home = jnp.stack([place_of(me, source_bits), place_of(me, target_bits), me])
    src_points = src_points.reshape(-1, size)
    tgt_message = pack(tgt_points.reshape(-1, size), g_init)
    late = [at for at in range(2, nc) if at & 1]
    early = [at for at in range(nc) if at not in late]
    ready = functools.partial(prepare, clusters=src_count, dims=dims, counts=(nr, nc))

    src_far = doubled(src_points, source_bits[1:])
    src_side = across(src_points, source_bits[0])
    tgt_far = doubled(tgt_message, target_bits[1:])
    held, home = lax.optimization_barrier((src_points, home))
    state = ready([(held, 0), (tgt_message, nr)], state=None)
    code = cand_owner * tgt_count + cand_local
    code, state, tgt_held = lax.optimization_barrier((code, state, tgt_message))
    tgt_side = across(tgt_held, target_bits[0])
    cand = lax.all_gather(code, "src", axis_index_groups=groups(source_bits)).reshape(sources, per_cluster)
    pairs = list_pairs(home, cand, target_bits, tgt_count, early, late)
    src_far[1:], cand = lax.optimization_barrier((src_far[1:], cand))

    def interleaved(far, side, bit):
        return [b for pair in zip(far, [side] + [across(block, bit) for block in far[1:]]) for b in pair]

    src_blocks = interleaved(src_far, src_side, source_bits[0])
    tgt_blocks = interleaved(tgt_far, tgt_side, target_bits[0])

    def pairs_of(sources_at, targets_at):
        return [(src_blocks[at], at) for at in sources_at] + [(tgt_blocks[at], nr + at) for at in targets_at]

    state = ready(pairs_of([], early[1:2]) + pairs_of(range(1, 2), early[2:]) + pairs_of(range(2, nr), []), state=state)

    def flat(state):
        return [a.reshape((-1,) + a.shape[2:]) for a in state]

    f32 = jnp.float32
    tiles = src_count * per_cluster
    for iteration in range(ITERS):
        first = iteration == 0
        if first:
            known = [(at * tgt_count, (at + 1) * tgt_count) for at in early]
            *operands, pot = flat(state)
            before = run_pass(
                functools.partial(first_row_kernel, sources, known),
                jax.ShapeDtypeStruct((2, sources, size), f32),
                pairs, operands, targets, sources, tiles, far_src, pot,
            )
            for at in late:
                state = ready(pairs_of([], [at]), state=state, after=(before,))
            *state, pot = flat(state)
            sums = run_pass(
                functools.partial(first_row_kernel, sources, None),
                jax.ShapeDtypeStruct((sources, size), f32),
                pairs, state, targets, sources, tiles, far_src, pot, before,
            )
        else:
            sums = run_pass(
                functools.partial(row_kernel, terms, sources),
                jax.ShapeDtypeStruct((sources, size), f32),
                pairs, state, targets, sources, tiles, far_src, sums,
            )
        sums = lax.all_gather(sums, "src", axis_index_groups=groups(source_bits))
        last = iteration + 1 == ITERS
        shapes = [jax.ShapeDtypeStruct((targets, size) if last else (nc, targets, size), f32)]
        shapes += [jax.ShapeDtypeStruct((src_count, size), f32)] if last else []
        column, *src_pot = run_pass(
            functools.partial(column_kernel, terms, sources, first, last),
            shapes,
            pairs, state, sources, targets, tiles, far_tgt, sums,
            scratch=(pltpu.VMEM((src_count, size), f32), pltpu.SemaphoreType.DMA),
        )
        if not last:
            sums = lax.all_to_all(column, "src", 0, 0, tiled=True, axis_index_groups=groups(target_bits))
    column = lax.all_to_all(
        column.reshape(nc, tgt_count, size), "src", 0, 0, tiled=True, axis_index_groups=groups(target_bits)
    )
    tgt_pot = -KEEP_TAU * SCALE_EPS * (jnp.log(sum(column[at] for at in range(nc))) - column_offset(terms))
    return (src_pot[0], tgt_pot)


def solution(mesh):
    return jax.shard_map(
        per_device,
        mesh=mesh,
        in_specs=(
            P(("groups", "src"), None, None),
            P(("groups", "src"), None, None),
            P(("groups", "src"), None),
            P(("groups", "src"), None),
            P(("groups", "src"), None),
            P(("groups", "src"), None),
            P(("groups", "src"), None),
        ),
        out_specs=(P(("groups", "src"), None), P(("groups", "src"), None)),
        check_vma=False,
    )
```
